32 devices in a mesh: row: 4 (over y, x), blk: 8 (over z, core).
Axes of the slice: x: 2, y: 2, z: 4, core: 2. Of those that a mesh axis runs over, the one named last changes fastest.
Arguments:
- features: bfloat16 [8192, 512], P(('row', 'blk')), may hold values from -6 to 6
- edge_tiles: bfloat16 [4, 8, 48, 128, 128], P('row', 'blk'), may hold values from 0 to 1
- tile_src: int32 [4, 8, 48], P('row', 'blk'), may hold values from 0 to 15, as said below
- tile_dst: int32 [4, 8, 48], P('row', 'blk'), may hold values from 0 to 7
- tile_count: int32 [4, 8], P('row', 'blk'), may hold values from 9 to 48, as said below
- weight: bfloat16 [1024, 512], replicated, may hold values from -0.25 to 0.25
- out_bias: float32 [512], replicated, may hold values from -3 to 3
Outputs:
- exposure: bfloat16 [8192, 512], P(('row', 'blk'))
The draws below stay inside these ranges and needn't reach their ends.
Inputs may be any that keep to these rules, and one draw needn't show every extreme that they name: `tile_count`: live slots of a device; the busiest device has all 48. `tile_src`: the live entries of each device ascend; source block s lies at loop position s // 2, which may be any position of the closed loop of 8 positions.
All inputs are finite; a program needn't handle non-finite values.
Results may differ from the reference program's by a relative error of at most 0.006.
Values may be sent and summed in bfloat16 or wider, within the bound.
A program may use at most 128 MiB of HBM per device.

```python
import math
import jax
import jax.numpy as jnp
from jax import lax

F = 512
BLOCK = 128
NB = 2
TILES_DEV = 48
GROUPS = 4
LOOP = 8
REACH = 4
NODES = 8192


def count_helper(key):
    divisor = jax.random.randint(jax.random.fold_in(key, 11), (GROUPS * LOOP,), 1, 6)
    counts = jnp.maximum(TILES_DEV // divisor, 2)
    chosen = jax.random.randint(jax.random.fold_in(key, 12), (), 0, GROUPS * LOOP)
    counts = jnp.where(jnp.arange(GROUPS * LOOP) == chosen, TILES_DEV, counts)
    return counts.reshape(GROUPS, LOOP).astype(jnp.int32)


def draw_tile_count(key, part):
    return count_helper(key)


def draw_tile_src(key, part):
    shape = (GROUPS, LOOP, TILES_DEV)
    offsets = jax.random.randint(jax.random.fold_in(key, 31), shape, -REACH, REACH + 1)
    slot_ids = jnp.arange(TILES_DEV)[None, None, :]
    offsets = jnp.where(slot_ids == 0, -REACH, jnp.where(slot_ids == 1, REACH, offsets))
    inner = jax.random.randint(jax.random.fold_in(key, 32), shape, 0, NB)
    position = (jnp.arange(LOOP)[None, :, None] + offsets) % LOOP
    sources = position * NB + inner
    counts = count_helper(key)
    live_slot = slot_ids < counts[:, :, None]
    ranked = jnp.where(live_slot, 0, LOOP * NB) + sources
    ordered = jnp.sort(ranked, axis=-1) % (LOOP * NB)
    return ordered.astype(jnp.int32)


def draw_edge_tiles(key, part):
    shape = (GROUPS, LOOP, TILES_DEV, BLOCK, BLOCK)
    activity = jnp.exp(jax.random.uniform(jax.random.fold_in(key, 21), (BLOCK,), jnp.float32, math.log(0.01), 0.0))
    picker = jax.random.uniform(jax.random.fold_in(key, 22), shape, jnp.float32)
    values = jnp.exp(jax.random.uniform(jax.random.fold_in(key, 23), shape, jnp.float32, math.log(0.1), 0.0))
    present = picker < 0.03 * activity[None, None, None, :, None]
    weights = jnp.where(present, values, 0.0)
    counts = count_helper(key)
    slot_ids = jnp.arange(TILES_DEV)[None, None, :, None, None]
    filled = jnp.where(slot_ids < counts[:, :, None, None, None], weights, 1.0 - picker)
    return filled.astype(jnp.bfloat16)


def place_ends(values, own_key, least, top_value):
    longest = values.shape.index(max(values.shape))
    spots = []
    for shift in (0, 1):
        where = [jax.random.randint(jax.random.fold_in(own_key, axis), (), 0, length) for axis, length in enumerate(values.shape)]
        where[longest] = (where[longest] + shift) % values.shape[longest]
        spots.append(tuple(where))
    return values.at[spots[0]].set(least).at[spots[1]].set(top_value)


def shard_levels(stream_key, extent, shards, least, top_value):
    factor_of = 1.0
    for axis_at, shards_of in shards:
        heights = jax.random.uniform(jax.random.fold_in(jax.random.fold_in(stream_key, 6), axis_at), (shards_of,), jnp.float32, least / len(shards), top_value / len(shards))
        factor_of = factor_of * jnp.repeat(jnp.exp(heights), extent[axis_at] // shards_of).reshape((-1,) + (1,) * (len(extent) - 1 - axis_at))
    return factor_of


def bell_draw(key, extent, width, limit, cuts=(), kind=jnp.bfloat16):
    values = jax.random.normal(key, extent, jnp.float32) * width
    if len(cuts) > 0:
        values = shard_levels(key, extent, cuts, -0.22, 0.18) * values
    return jnp.clip(values, min=-limit, max=limit).astype(kind)


def setup_inputs(seed: int = 0) -> dict:
    arg_keys = jax.random.split(jax.random.key(seed), 8)
    return {
        "features": bell_draw(arg_keys[0], (NODES, F), 1.0, 6.0, ((0, 32),)),
        "edge_tiles": draw_edge_tiles(jax.random.fold_in(arg_keys[7], 71), 0),
        "tile_src": draw_tile_src(jax.random.fold_in(arg_keys[7], 71), 0),
        "tile_dst": place_ends(jax.random.randint(arg_keys[3], (GROUPS, LOOP, TILES_DEV), 0, GROUPS * NB), jax.random.fold_in(arg_keys[3], 1), 0, (GROUPS * NB) - 1).astype(jnp.int32),
        "tile_count": draw_tile_count(jax.random.fold_in(arg_keys[7], 71), 0),
        "weight": bell_draw(arg_keys[5], (2 * F, F), F ** -0.5, 0.25),
        "out_bias": bell_draw(arg_keys[6], (F,), 0.5, 3.0, (), jnp.float32),
    }


def reference(features, edge_tiles, tile_src, tile_dst, tile_count, weight, out_bias):
    tile_width = edge_tiles.shape[-1]
    feat_width = features.shape[1]
    dest_blocks = GROUPS * NB
    feat_blocks = features.reshape(GROUPS, LOOP * NB, tile_width, feat_width)
    block_ids = jnp.arange(dest_blocks, dtype=jnp.int32)
    slot_ids = jnp.arange(TILES_DEV, dtype=jnp.int32)

    def device_step(carry, index):
        totals, degrees = carry
        group = index // LOOP
        column = index % LOOP
        tiles_here = edge_tiles[group, column]
        sources = tile_src[group, column]
        targets = tile_dst[group, column]
        live_slot = slot_ids < tile_count[group, column]
        gathered = feat_blocks[group][sources]
        products = jnp.einsum("tij,tjf->tif", tiles_here.astype(jnp.float32), gathered.astype(jnp.float32), precision=lax.Precision.HIGHEST)
        selector = ((targets[None, :] == block_ids[:, None]) & live_slot[None, :]).astype(jnp.float32)
        partial_value = jnp.einsum("qt,tif->qif", selector, products, precision=lax.Precision.HIGHEST).astype(jnp.bfloat16)
        row_sums = jnp.sum(tiles_here, axis=2, dtype=jnp.float32)
        partial_degree = jnp.dot(selector, row_sums, precision=lax.Precision.HIGHEST).astype(jnp.bfloat16)
        totals = totals.at[column].add(partial_value.astype(jnp.float32))
        degrees = degrees.at[column].add(partial_degree.astype(jnp.float32))
        return (totals, degrees), None

    start_totals = jnp.zeros((LOOP, dest_blocks, tile_width, feat_width), jnp.float32)
    start_degrees = jnp.zeros((LOOP, dest_blocks, tile_width), jnp.float32)
    (totals, degrees), unused = lax.scan(device_step, (start_totals, start_degrees), jnp.arange(GROUPS * LOOP, dtype=jnp.int32))
    aggregate = totals.reshape(LOOP, GROUPS, NB, tile_width, feat_width).transpose(1, 0, 2, 3, 4).reshape(-1, feat_width)
    degree = degrees.reshape(LOOP, GROUPS, NB, tile_width).transpose(1, 0, 2, 3).reshape(-1)
    neighbor_mean = (aggregate / jnp.maximum(degree, 1.0)[:, None]).astype(jnp.bfloat16)
    joined = jnp.concatenate([features, neighbor_mean], axis=1)
    mixed = jnp.dot(joined, weight, preferred_element_type=jnp.float32) + out_bias
    return jax.nn.relu(mixed).astype(jnp.bfloat16)
```

```python
import functools

import jax
import jax.numpy as jnp
from jax import lax
from jax.experimental import pallas as pl
from jax.experimental.pallas import tpu as pltpu
from jax.sharding import PartitionSpec as P

MESH = pl.DeviceIdType.MESH
CHUNK = 128
AHEAD = 3
DENSE_LIMIT = 12 * 2**20


def fused(
    rows_n, spots, live_ref, src_ref, dst_ref, feat_hbm, tiles_hbm, weight_hbm, bias_ref, out_ref,
    tab, tiles, chain, dense, weight, mine, acc, mixed, send_buf, recv_buf, lists, list_smem,
    in_sem, own_sem, left_sem, right_sem, side_sem, line_recv, side_recv, row_send, row_recv,
):
    slots = tiles.shape[0]
    width = tiles.shape[-1]
    chunks = tab.shape[0]
    node_rows = mine.shape[0]
    feat = mine.shape[1]
    per_node = node_rows // width
    sources = spots * 2 * per_node
    dests = rows_n * per_node
    wide = 2 * per_node
    row = lax.axis_index("row")
    blk = lax.axis_index("blk")
    z = blk // 2
    c = blk % 2
    side = z * 2 + (1 - c)

    loads = [
        pltpu.make_async_copy(tiles_hbm, tiles, in_sem.at[0]),
        pltpu.make_async_copy(feat_hbm, mine, in_sem.at[1]),
        pltpu.make_async_copy(weight_hbm, weight, in_sem.at[2]),
    ]
    for load in loads:
        load.start()

    barrier = pltpu.get_barrier_semaphore()

    def greet(r, b):
        pl.semaphore_signal(barrier, inc=1, device_id=(r, b), device_id_type=MESH)

    @pl.when(z > 0)
    def _():
        greet(row, blk - 2)

    @pl.when(z < spots - 1)
    def _():
        greet(row, blk + 2)

    greet(row, side)
    for step in range(1, rows_n):
        greet((row + step) % rows_n, blk)

    def own_local(k):
        return pltpu.make_async_copy(
            feat_hbm.at[:, pl.ds(pl.multiple_of(k * CHUNK, CHUNK), CHUNK)], tab.at[k, z, c], own_sem.at[k]
        )

    def line_copy(k, p, step, sems, own):
        slot = tab.at[k, p, c]
        source = feat_hbm.at[:, pl.ds(pl.multiple_of(k * CHUNK, CHUNK), CHUNK)] if own else slot
        return pltpu.make_async_remote_copy(
            src_ref=source, dst_ref=slot, send_sem=sems.at[k, p], recv_sem=line_recv.at[k, p],
            device_id=(row, blk + 2 * step), device_id_type=MESH,
        )

    def side_copy(k, p, own):
        slot = tab.at[k, p, c]
        source = feat_hbm.at[:, pl.ds(pl.multiple_of(k * CHUNK, CHUNK), CHUNK)] if own else slot
        return pltpu.make_async_remote_copy(
            src_ref=source, dst_ref=slot, send_sem=side_sem.at[k, p], recv_sem=side_recv.at[k, p],
            device_id=(row, side), device_id_type=MESH,
        )

    def side_arrival(k, p):
        slot = tab.at[k, p, 1 - c]
        return pltpu.make_async_remote_copy(
            src_ref=slot, dst_ref=slot, send_sem=side_sem.at[k, p], recv_sem=side_recv.at[k, p],
            device_id=(row, side), device_id_type=MESH,
        )

    def row_copy(k, step):
        peer = (row + step) % rows_n
        return pltpu.make_async_remote_copy(
            src_ref=send_buf.at[k, peer], dst_ref=recv_buf.at[k, row],
            send_sem=row_send.at[k, peer], recv_sem=row_recv.at[k, row],
            device_id=(peer, blk), device_id_type=MESH,
        )

    def row_arrival(k, step):
        peer = (row + step) % rows_n
        return pltpu.make_async_remote_copy(
            src_ref=send_buf.at[k, peer], dst_ref=recv_buf.at[k, peer],
            send_sem=row_send.at[k, peer], recv_sem=row_recv.at[k, peer],
            device_id=(peer, blk), device_id_type=MESH,
        )

    def send_own(k):
        @pl.when(z > 0)
        def _():
            line_copy(k, z, -1, left_sem, True).start()

        @pl.when(z < spots - 1)
        def _():
            line_copy(k, z, 1, right_sem, True).start()

        side_copy(k, z, True).start()

    greeted = (
        jnp.where(z > 0, 1, 0) + jnp.where(z < spots - 1, 1, 0) + rows_n
    )
    pl.semaphore_wait(barrier, greeted)

    def first_sends(k, carry):
        send_own(k)
        own_local(k).start()
        return carry

    lax.fori_loop(0, min(AHEAD, chunks), first_sends, 0)

    list_rows = lists.shape[0] - 1
    lane = lax.broadcasted_iota(jnp.int32, (1, 128), 1)
    place = lax.broadcasted_iota(jnp.int32, (list_rows, 128), 0) * 128 + lax.broadcasted_iota(
        jnp.int32, (list_rows, 128), 1
    )
    live = live_ref[0, 0]

    def one_key(t, carry):
        keys, last = carry
        key = dst_ref[0, t] * sources + src_ref[0, t]
        key = jnp.where(t < live, key, -1)
        return jnp.where(lane == t, key, keys), jnp.where(place == key, t, last)

    keys, last = lax.fori_loop(
        0, slots, one_key,
        (jnp.full((1, 128), -1, jnp.int32), jnp.full((list_rows, 128), slots, jnp.int32)), unroll=8,
    )

    def one_before(u, before):
        key = dst_ref[0, u] * sources + src_ref[0, u]
        key = jnp.where(u < live, key, -2)
        return jnp.where((keys == key) & (lane > u), u, before)

    before = lax.fori_loop(0, slots, one_before, jnp.full((1, 128), slots, jnp.int32), unroll=8)
    lists[pl.ds(0, list_rows), :] = last
    lists[pl.ds(list_rows, 1), :] = before
    to_smem = pltpu.make_async_copy(lists, list_smem, in_sem.at[3])
    to_smem.start()
    chain[slots] = jnp.zeros((width, width), jnp.float32)
    loads[0].wait()
    to_smem.wait()

    def one_link(t, carry):
        chain[t] = tiles[t].astype(jnp.float32) + chain[list_smem[list_rows, t]]
        return carry

    lax.fori_loop(0, slots, one_link, 0, unroll=4)

    def one_dest(q, carry):
        for s in range(sources):
            at = q * sources + s
            block = chain[list_smem[at // 128, at % 128]]
            dense[s // wide, pl.ds(pl.multiple_of(q * width, width), width), pl.ds(s % wide * width, width)] = (
                block.astype(jnp.bfloat16)
            )
        return carry

    lax.fori_loop(0, dests, one_dest, 0)

    def consume(k, p, first):
        block = tab[k, p].reshape(wide * width, CHUNK)
        product = jnp.dot(dense[p], block, preferred_element_type=jnp.float32)
        if first:
            acc[k] = product
        else:
            acc[k] += product

    def send_rows(k, values):
        send_buf[k] = values.astype(jnp.bfloat16).reshape(rows_n, node_rows, CHUNK)
        for step in range(1, rows_n):
            row_copy(k, step).start()

    def gather_rows(k):
        total = send_buf[k, row].astype(jnp.float32)
        for step in range(1, rows_n):
            row_arrival(k, step).wait_recv()
            total += recv_buf[k, (row + step) % rows_n].astype(jnp.float32)
        return total

    def step_body(s, carry):
        @pl.when(s + AHEAD < chunks)
        def _():
            send_own(s + AHEAD)
            own_local(s + AHEAD).start()

        for h in range(1, spots):
            k = s - (h - 1)
            inside = (k >= 0) & (k < chunks)

            @pl.when(inside & (z + h < spots))
            def _():
                line_copy(k, z + h, -1, left_sem, False).wait_recv()

                @pl.when(z > 0)
                def _():
                    line_copy(k, z + h, -1, left_sem, False).start()

                side_copy(k, z + h, False).start()

            @pl.when(inside & (z - h >= 0))
            def _():
                line_copy(k, z - h, 1, right_sem, False).wait_recv()

                @pl.when(z < spots - 1)
                def _():
                    line_copy(k, z - h, 1, right_sem, False).start()

                side_copy(k, z - h, False).start()

        @pl.when(s == 0)
        def _():
            ones = jnp.ones((wide * width, CHUNK), jnp.bfloat16)
            total = jnp.dot(dense[0], ones, preferred_element_type=jnp.float32)
            for p in range(1, spots):
                total += jnp.dot(dense[p], ones, preferred_element_type=jnp.float32)
            send_rows(chunks, total)

        @pl.when(s == 1)
        def _():
            loads[1].wait()
            loads[2].wait()
            mixed[...] = (
                jnp.dot(mine[...], weight[pl.ds(0, feat), :], preferred_element_type=jnp.float32) + bias_ref[...]
            )

        for h in range(spots):
            k = s - h
            inside = (k >= 0) & (k < chunks)
            if h == 0:

                @pl.when(inside)
                def _():
                    own_local(k).wait()
                    side_arrival(k, z).wait_recv()
                    consume(k, z, True)

            else:

                @pl.when(inside & (z + h < spots))
                def _():
                    side_arrival(k, z + h).wait_recv()
                    consume(k, z + h, False)

                @pl.when(inside & (z - h >= 0))
                def _():
                    side_arrival(k, z - h).wait_recv()
                    consume(k, z - h, False)

        ready = s - (spots - 1)

        @pl.when((ready >= 0) & (ready < chunks))
        def _():
            send_rows(ready, acc[ready])

        arrived = s - spots

        @pl.when(arrived == 0)
        def _():
            acc[0, pl.ds(0, node_rows), :] = jnp.maximum(gather_rows(chunks), 1.0)

        @pl.when(arrived >= 0)
        def _():
            mean = (gather_rows(arrived) / acc[0, pl.ds(0, node_rows), :]).astype(jnp.bfloat16)
            part = weight[pl.ds(pl.multiple_of(feat + arrived * CHUNK, CHUNK), CHUNK), :]
            mixed[...] += jnp.dot(mean, part, preferred_element_type=jnp.float32)

        return carry

    lax.fori_loop(0, chunks + spots, step_body, 0)
    out_ref[...] = jnp.maximum(mixed[...], 0.0).astype(jnp.bfloat16)

    def finish(k, carry):
        side_copy(k, z, True).wait_send()

        @pl.when(z > 0)
        def _():
            line_copy(k, z, -1, left_sem, True).wait_send()

        @pl.when(z < spots - 1)
        def _():
            line_copy(k, z, 1, right_sem, True).wait_send()

        for h in range(1, spots):

            @pl.when(z + h < spots)
            def _():
                side_copy(k, z + h, False).wait_send()

                @pl.when(z > 0)
                def _():
                    line_copy(k, z + h, -1, left_sem, False).wait_send()

            @pl.when(z - h >= 0)
            def _():
                side_copy(k, z - h, False).wait_send()

                @pl.when(z < spots - 1)
                def _():
                    line_copy(k, z - h, 1, right_sem, False).wait_send()

        return carry

    lax.fori_loop(0, chunks, finish, 0)

    def finish_rows(k, carry):
        for step in range(1, rows_n):
            row_copy(k, step).wait_send()
        return carry

    lax.fori_loop(0, chunks + 1, finish_rows, 0)


def per_device_fused(features, edge_tiles, tile_src, tile_dst, tile_count, weight, out_bias):
    rows_n = lax.axis_size("row")
    spots = lax.axis_size("blk") // 2
    slots, width = edge_tiles.shape[2], edge_tiles.shape[-1]
    node_rows, feat = features.shape
    chunks = feat // CHUNK
    per_node = node_rows // width
    dests, sources = rows_n * per_node, spots * 2 * per_node
    list_rows = -(-dests * sources // 128)
    dest_rows = rows_n * node_rows
    hbm = pl.BlockSpec(memory_space=pl.ANY)
    smem = pl.BlockSpec(memory_space=pltpu.SMEM)
    vmem = pl.BlockSpec(memory_space=pltpu.VMEM)
    dma = pltpu.SemaphoreType.DMA
    return pl.pallas_call(
        functools.partial(fused, rows_n, spots),
        out_shape=jax.ShapeDtypeStruct((node_rows, feat), jnp.bfloat16),
        in_specs=[smem, smem, smem, hbm, hbm, hbm, vmem],
        out_specs=vmem,
        scratch_shapes=[
            pltpu.VMEM((chunks, spots, 2, node_rows, CHUNK), jnp.bfloat16),
            pltpu.VMEM((slots, width, width), jnp.bfloat16),
            pltpu.VMEM((slots + 1, width, width), jnp.float32),
            pltpu.VMEM((spots, dest_rows, 2 * node_rows), jnp.bfloat16),
            pltpu.VMEM(weight.shape, jnp.bfloat16),
            pltpu.VMEM((node_rows, feat), jnp.bfloat16),
            pltpu.VMEM((chunks, dest_rows, CHUNK), jnp.float32),
            pltpu.VMEM((node_rows, feat), jnp.float32),
            pltpu.VMEM((chunks + 1, rows_n, node_rows, CHUNK), jnp.bfloat16),
            pltpu.VMEM((chunks + 1, rows_n, node_rows, CHUNK), jnp.bfloat16),
            pltpu.VMEM((list_rows + 1, 128), jnp.int32),
            pltpu.SMEM((list_rows + 1, 128), jnp.int32),
            dma((4,)),
            dma((chunks,)),
            dma((chunks, spots)),
            dma((chunks, spots)),
            dma((chunks, spots)),
            dma((chunks, spots)),
            dma((chunks, spots)),
            dma((chunks + 1, rows_n)),
            dma((chunks + 1, rows_n)),
        ],
        compiler_params=pltpu.CompilerParams(
            collective_id=0, has_side_effects=True, vmem_limit_bytes=48 * 2**20
        ),
    )(
        tile_count,
        tile_src.reshape(1, slots),
        tile_dst.reshape(1, slots),
        features,
        edge_tiles.reshape(slots, width, width),
        weight,
        out_bias.reshape(1, feat),
    )


def accumulate(table, block_of, tiles_here, target_ids, live_slot, dest_blocks):
    slot_total = tiles_here.shape[0]
    tile_width = tiles_here.shape[-1]
    feat_width = table.shape[1]
    table_blocks = table.reshape(-1, tile_width, feat_width)
    source_total = table_blocks.shape[0]
    step_size = 16
    rounds = slot_total // step_size
    source_ids = jnp.arange(source_total, dtype=jnp.int32)
    dest_ids = jnp.arange(dest_blocks, dtype=jnp.int32)

    def one_round(index, totals):
        first = index * step_size
        tiles = lax.dynamic_slice_in_dim(tiles_here, first, step_size, 0)
        blocks = lax.dynamic_slice_in_dim(block_of, first, step_size, 0)
        targets = lax.dynamic_slice_in_dim(target_ids, first, step_size, 0)
        live = lax.dynamic_slice_in_dim(live_slot, first, step_size, 0)
        one_hot = (blocks[:, None] == source_ids[None, :]).astype(jnp.bfloat16)
        picked = jnp.einsum(
            "tk,kif->tif", one_hot, table_blocks, preferred_element_type=jnp.float32
        ).astype(jnp.bfloat16)
        products = jnp.einsum("tij,tjf->tif", tiles, picked, preferred_element_type=jnp.float32)
        selector = ((targets[None, :] == dest_ids[:, None]) & live[None, :]).astype(jnp.float32)
        return totals + jnp.einsum(
            "qt,tif->qif", selector, products, precision=lax.Precision.HIGHEST
        )

    empty = jnp.zeros((dest_blocks, tile_width, feat_width), jnp.float32)
    return lax.fori_loop(0, rounds, one_round, empty)


def per_device(features, edge_tiles, tile_src, tile_dst, tile_count, weight, out_bias):
    tiles_here = edge_tiles[0, 0]
    source_ids = tile_src[0, 0]
    target_ids = tile_dst[0, 0]
    live_count = tile_count[0, 0]
    slot_total = tiles_here.shape[0]
    tile_width = tiles_here.shape[-1]
    node_rows = features.shape[0]
    feat_width = features.shape[1]
    group_count = lax.axis_size("row")
    dest_blocks = group_count * node_rows // tile_width
    slot_ids = jnp.arange(slot_total, dtype=jnp.int32)
    live_slot = slot_ids < live_count
    table = lax.all_gather(features, "blk", axis=0, tiled=True)
    totals = accumulate(table, source_ids, tiles_here, target_ids, live_slot, dest_blocks).reshape(
        -1, feat_width
    )
    row_sums = jnp.sum(tiles_here, axis=2, dtype=jnp.float32)
    block_ids = jnp.arange(dest_blocks, dtype=jnp.int32)
    selector = ((target_ids[None, :] == block_ids[:, None]) & live_slot[None, :]).astype(
        jnp.float32
    )
    degree_part = jnp.dot(selector, row_sums, precision=lax.Precision.HIGHEST).reshape(-1)
    aggregate, degree = (
        lax.psum_scatter(
            totals.astype(jnp.bfloat16), "row", scatter_dimension=0, tiled=True
        ).astype(jnp.float32),
        lax.psum_scatter(
            degree_part.astype(jnp.bfloat16), "row", scatter_dimension=0, tiled=True
        ).astype(jnp.float32),
    )
    neighbor_mean = (aggregate / jnp.maximum(degree, 1.0)[:, None]).astype(jnp.bfloat16)
    joined = jnp.concatenate([features, neighbor_mean], axis=1)
    mixed = jnp.dot(joined, weight, preferred_element_type=jnp.float32) + out_bias
    return jax.nn.relu(mixed).astype(jnp.bfloat16)


def solution(mesh):
    in_specs = (
        P(("row", "blk"), None),
        P("row", "blk", None, None, None),
        P("row", "blk", None),
        P("row", "blk", None),
        P("row", "blk"),
        P(),
        P(),
    )
    out_specs = P(("row", "blk"), None)

    def body(features, edge_tiles, *rest):
        dense = 2 * lax.axis_size("row") * lax.axis_size("blk") * features.shape[0] ** 2
        run = per_device_fused if dense <= DENSE_LIMIT else per_device
        return run(features, edge_tiles, *rest)

    return jax.shard_map(
        body, mesh=mesh, in_specs=in_specs, out_specs=out_specs, check_vma=False
    )
```

```python
import functools

import jax
import jax.numpy as jnp
from jax import lax
from jax.experimental import pallas as pl
from jax.experimental.pallas import tpu as pltpu
from jax.sharding import PartitionSpec as P

MESH = pl.DeviceIdType.MESH
CHUNK = 128
AHEAD = 3
DENSE_LIMIT = 12 * 2**20


def fused(
    rows_n, spots, live_hbm, src_hbm, dst_hbm, feat_hbm, tiles_hbm, weight_hbm, bias_hbm, out_ref,
    live_ref, src_ref, dst_ref, bias_ref, tab, tiles, chain, dense, weight, mine, acc, mixed, degree, send_buf, recv_buf, lists, list_smem,
    in_sem, own_sem, left_sem, right_sem, side_sem, line_recv, side_recv, row_send, row_recv,
):
    slots = tiles.shape[0]
    width = tiles.shape[-1]
    chunks = tab.shape[0]
    node_rows = mine.shape[0]
    feat = mine.shape[1]
    per_node = node_rows // width
    sources = spots * 2 * per_node
    dests = rows_n * per_node
    wide = 2 * per_node
    row = lax.axis_index("row")
    blk = lax.axis_index("blk")
    z = blk // 2
    c = blk % 2
    side = z * 2 + (1 - c)

    barrier = pltpu.get_barrier_semaphore()

    def greet(r, b):
        pl.semaphore_signal(barrier, inc=1, device_id=(r, b), device_id_type=MESH)

    @pl.when(z > 0)
    def _():
        greet(row, blk - 2)

    @pl.when(z < spots - 1)
    def _():
        greet(row, blk + 2)

    greet(row, side)
    for step in range(1, rows_n):
        greet((row + step) % rows_n, blk)

    def own_local(k):
        return pltpu.make_async_copy(
            feat_hbm.at[:, pl.ds(pl.multiple_of(k * CHUNK, CHUNK), CHUNK)], tab.at[k, z, c], own_sem.at[k]
        )

    def line_copy(k, p, step, sems, own):
        slot = tab.at[k, p, c]
        source = feat_hbm.at[:, pl.ds(pl.multiple_of(k * CHUNK, CHUNK), CHUNK)] if own else slot
        return pltpu.make_async_remote_copy(
            src_ref=source, dst_ref=slot, send_sem=sems.at[k, p], recv_sem=line_recv.at[k, p],
            device_id=(row, blk + 2 * step), device_id_type=MESH,
        )

    def side_copy(k, p, own):
        slot = tab.at[k, p, c]
        source = feat_hbm.at[:, pl.ds(pl.multiple_of(k * CHUNK, CHUNK), CHUNK)] if own else slot
        return pltpu.make_async_remote_copy(
            src_ref=source, dst_ref=slot, send_sem=side_sem.at[k, p], recv_sem=side_recv.at[k, p],
            device_id=(row, side), device_id_type=MESH,
        )

    def side_arrival(k, p):
        slot = tab.at[k, p, 1 - c]
        return pltpu.make_async_remote_copy(
            src_ref=slot, dst_ref=slot, send_sem=side_sem.at[k, p], recv_sem=side_recv.at[k, p],
            device_id=(row, side), device_id_type=MESH,
        )

    def row_copy(k, step):
        peer = (row + step) % rows_n
        return pltpu.make_async_remote_copy(
            src_ref=send_buf.at[k, peer], dst_ref=recv_buf.at[k, row],
            send_sem=row_send.at[k, peer], recv_sem=row_recv.at[k, row],
            device_id=(peer, blk), device_id_type=MESH,
        )

    def row_arrival(k, step):
        peer = (row + step) % rows_n
        return pltpu.make_async_remote_copy(
            src_ref=send_buf.at[k, peer], dst_ref=recv_buf.at[k, peer],
            send_sem=row_send.at[k, peer], recv_sem=row_recv.at[k, peer],
            device_id=(peer, blk), device_id_type=MESH,
        )

    def send_own(k):
        @pl.when(z > 0)
        def _():
            line_copy(k, z, -1, left_sem, True).start()

        @pl.when(z < spots - 1)
        def _():
            line_copy(k, z, 1, right_sem, True).start()

        side_copy(k, z, True).start()

    loads = [
        pltpu.make_async_copy(tiles_hbm, tiles, in_sem.at[0]),
        pltpu.make_async_copy(feat_hbm, mine, in_sem.at[1]),
        pltpu.make_async_copy(weight_hbm, weight, in_sem.at[2]),
        pltpu.make_async_copy(bias_hbm, bias_ref, in_sem.at[4]),
        pltpu.make_async_copy(live_hbm, live_ref, in_sem.at[5]),
        pltpu.make_async_copy(src_hbm, src_ref, in_sem.at[6]),
        pltpu.make_async_copy(dst_hbm, dst_ref, in_sem.at[7]),
    ]
    for load in loads[4:] + loads[:1]:
        load.start()

    greeted = (
        jnp.where(z > 0, 1, 0) + jnp.where(z < spots - 1, 1, 0) + rows_n
    )
    pl.semaphore_wait(barrier, greeted)

    def first_sends(k, carry):
        send_own(k)
        own_local(k).start()
        return carry

    lax.fori_loop(0, min(AHEAD, chunks), first_sends, 0)
    for load in loads[1:4]:
        load.start()
    for load in loads[4:]:
        load.wait()

    list_rows = lists.shape[0] - 1
    lane = lax.broadcasted_iota(jnp.int32, (1, 128), 1)
    place = lax.broadcasted_iota(jnp.int32, (list_rows, 128), 0) * 128 + lax.broadcasted_iota(
        jnp.int32, (list_rows, 128), 1
    )
    live = live_ref[0, 0]

    def one_key(t, carry):
        keys, last = carry
        key = dst_ref[0, 0, t] * sources + src_ref[0, 0, t]
        key = jnp.where(t < live, key, -1)
        return jnp.where(lane == t, key, keys), jnp.where(place == key, t, last)

    keys, last = lax.fori_loop(
        0, slots, one_key,
        (jnp.full((1, 128), -1, jnp.int32), jnp.full((list_rows, 128), slots, jnp.int32)), unroll=8,
    )

    def one_before(u, before):
        key = dst_ref[0, 0, u] * sources + src_ref[0, 0, u]
        key = jnp.where(u < live, key, -2)
        return jnp.where((keys == key) & (lane > u), u, before)

    before = lax.fori_loop(0, slots, one_before, jnp.full((1, 128), slots, jnp.int32), unroll=8)
    lists[pl.ds(0, list_rows), :] = last
    lists[pl.ds(list_rows, 1), :] = before
    to_smem = pltpu.make_async_copy(lists, list_smem, in_sem.at[3])
    to_smem.start()
    chain[slots] = jnp.zeros((width, width), jnp.float32)
    loads[0].wait()
    to_smem.wait()

    def one_link(t, carry):
        chain[t] = tiles[t].astype(jnp.float32) + chain[list_smem[list_rows, t]]
        return carry

    lax.fori_loop(0, slots, one_link, 0, unroll=4)

    def one_dest(q, carry):
        for s in range(sources):
            at = q * sources + s
            block = chain[list_smem[at // 128, at % 128]]
            dense[s // wide, pl.ds(pl.multiple_of(q * width, width), width), pl.ds(s % wide * width, width)] = (
                block.astype(jnp.bfloat16)
            )
        return carry


    def consume(k, p, first):
        block = tab[k, p].reshape(wide * width, CHUNK)
        product = jnp.dot(dense[p], block, preferred_element_type=jnp.float32)
        if first:
            acc[k] = product
        else:
            acc[k] += product

    def send_rows(k, values):
        send_buf[k] = values.astype(jnp.bfloat16).reshape(rows_n, node_rows, CHUNK)
        for step in range(1, rows_n):
            row_copy(k, step).start()

    def gather_rows(k):
        total = send_buf[k, row].astype(jnp.float32)
        for step in range(1, rows_n):
            row_arrival(k, step).wait_recv()
            total += recv_buf[k, (row + step) % rows_n].astype(jnp.float32)
        return total

    def forward(k, h):
        @pl.when(z + h < spots)
        def _():
            line_copy(k, z + h, -1, left_sem, False).wait_recv()

            @pl.when(z > 0)
            def _():
                line_copy(k, z + h, -1, left_sem, False).start()

            side_copy(k, z + h, False).start()

        @pl.when(z - h >= 0)
        def _():
            line_copy(k, z - h, 1, right_sem, False).wait_recv()

            @pl.when(z < spots - 1)
            def _():
                line_copy(k, z - h, 1, right_sem, False).start()

            side_copy(k, z - h, False).start()

    def consume_at(k, h):
        if h == 0:
            own_local(k).wait()
            side_arrival(k, z).wait_recv()
            consume(k, z, True)
            return

        @pl.when(z + h < spots)
        def _():
            side_arrival(k, z + h).wait_recv()
            consume(k, z + h, False)

        @pl.when(z - h >= 0)
        def _():
            side_arrival(k, z - h).wait_recv()
            consume(k, z - h, False)

    def finish_mean(k):
        mean = (gather_rows(k) / degree[...]).astype(jnp.bfloat16)
        part = weight[pl.ds(pl.multiple_of(feat + k * CHUNK, CHUNK), CHUNK), :]
        mixed[...] += jnp.dot(mean, part, preferred_element_type=jnp.float32)

    def stage(k, carry):
        forward(k, 1)

        @pl.when(k + AHEAD < chunks)
        def _():
            send_own(k + AHEAD)
            own_local(k + AHEAD).start()

        @pl.when(k == 0)
        def _():
            lax.fori_loop(0, dests, one_dest, 0)

        for h in range(2, spots):
            forward(k, h)
            if h == 2:
                consume_at(k, 0)

                @pl.when(k == 0)
                def _():
                    ones = jnp.ones((wide * width, CHUNK), jnp.bfloat16)
                    total = jnp.dot(dense[0], ones, preferred_element_type=jnp.float32)
                    for p in range(1, spots):
                        total += jnp.dot(dense[p], ones, preferred_element_type=jnp.float32)
                    send_rows(chunks, total)

            consume_at(k, h - 1)
        consume_at(k, spots - 1)
        send_rows(k, acc[k])

        @pl.when(k == 0)
        def _():
            for load in loads[1:4]:
                load.wait()
            mixed[...] = (
                jnp.dot(mine[...], weight[pl.ds(0, feat), :], preferred_element_type=jnp.float32) + bias_ref[...]
            )
            degree[...] = jnp.maximum(gather_rows(chunks), 1.0)

        @pl.when(k > 0)
        def _():
            finish_mean(k - 1)

        return carry

    lax.fori_loop(0, chunks, stage, 0)
    finish_mean(chunks - 1)
    out_ref[...] = jnp.maximum(mixed[...], 0.0).astype(jnp.bfloat16)

    def finish(k, carry):
        side_copy(k, z, True).wait_send()

        @pl.when(z > 0)
        def _():
            line_copy(k, z, -1, left_sem, True).wait_send()

        @pl.when(z < spots - 1)
        def _():
            line_copy(k, z, 1, right_sem, True).wait_send()

        for h in range(1, spots):

            @pl.when(z + h < spots)
            def _():
                side_copy(k, z + h, False).wait_send()

                @pl.when(z > 0)
                def _():
                    line_copy(k, z + h, -1, left_sem, False).wait_send()

            @pl.when(z - h >= 0)
            def _():
                side_copy(k, z - h, False).wait_send()

                @pl.when(z < spots - 1)
                def _():
                    line_copy(k, z - h, 1, right_sem, False).wait_send()

        return carry

    lax.fori_loop(0, chunks, finish, 0)

    def finish_rows(k, carry):
        for step in range(1, rows_n):
            row_copy(k, step).wait_send()
        return carry

    lax.fori_loop(0, chunks + 1, finish_rows, 0)


def per_device_fused(features, edge_tiles, tile_src, tile_dst, tile_count, weight, out_bias):
    rows_n = lax.axis_size("row")
    spots = lax.axis_size("blk") // 2
    slots, width = edge_tiles.shape[2], edge_tiles.shape[-1]
    node_rows, feat = features.shape
    chunks = feat // CHUNK
    per_node = node_rows // width
    dests, sources = rows_n * per_node, spots * 2 * per_node
    list_rows = -(-dests * sources // 128)
    dest_rows = rows_n * node_rows
    hbm = pl.BlockSpec(memory_space=pltpu.HBM)
    vmem = pl.BlockSpec(memory_space=pltpu.VMEM)
    dma = pltpu.SemaphoreType.DMA
    return pl.pallas_call(
        functools.partial(fused, rows_n, spots),
        out_shape=jax.ShapeDtypeStruct((node_rows, feat), jnp.bfloat16),
        in_specs=[hbm] * 7,
        out_specs=vmem,
        scratch_shapes=[
            pltpu.SMEM(tile_count.shape, jnp.int32),
            pltpu.SMEM(tile_src.shape, jnp.int32),
            pltpu.SMEM(tile_dst.shape, jnp.int32),
            pltpu.VMEM((1, feat), jnp.float32),
            pltpu.VMEM((chunks, spots, 2, node_rows, CHUNK), jnp.bfloat16),
            pltpu.VMEM((slots, width, width), jnp.bfloat16),
            pltpu.VMEM((slots + 1, width, width), jnp.float32),
            pltpu.VMEM((spots, dest_rows, 2 * node_rows), jnp.bfloat16),
            pltpu.VMEM(weight.shape, jnp.bfloat16),
            pltpu.VMEM((node_rows, feat), jnp.bfloat16),
            pltpu.VMEM((chunks, dest_rows, CHUNK), jnp.float32),
            pltpu.VMEM((node_rows, feat), jnp.float32),
            pltpu.VMEM((node_rows, CHUNK), jnp.float32),
            pltpu.VMEM((chunks + 1, rows_n, node_rows, CHUNK), jnp.bfloat16),
            pltpu.VMEM((chunks + 1, rows_n, node_rows, CHUNK), jnp.bfloat16),
            pltpu.VMEM((list_rows + 1, 128), jnp.int32),
            pltpu.SMEM((list_rows + 1, 128), jnp.int32),
            dma((8,)),
            dma((chunks,)),
            dma((chunks, spots)),
            dma((chunks, spots)),
            dma((chunks, spots)),
            dma((chunks, spots)),
            dma((chunks, spots)),
            dma((chunks + 1, rows_n)),
            dma((chunks + 1, rows_n)),
        ],
        compiler_params=pltpu.CompilerParams(
            collective_id=0, has_side_effects=True, vmem_limit_bytes=60 * 2**20
        ),
    )(
        tile_count,
        tile_src,
        tile_dst,
        features,
        edge_tiles.reshape(slots, width, width),
        weight,
        out_bias.reshape(1, feat),
    )


def accumulate(table, block_of, tiles_here, target_ids, live_slot, dest_blocks):
    slot_total = tiles_here.shape[0]
    tile_width = tiles_here.shape[-1]
    feat_width = table.shape[1]
    table_blocks = table.reshape(-1, tile_width, feat_width)
    source_total = table_blocks.shape[0]
    step_size = 16
    rounds = slot_total // step_size
    source_ids = jnp.arange(source_total, dtype=jnp.int32)
    dest_ids = jnp.arange(dest_blocks, dtype=jnp.int32)

    def one_round(index, totals):
        first = index * step_size
        tiles = lax.dynamic_slice_in_dim(tiles_here, first, step_size, 0)
        blocks = lax.dynamic_slice_in_dim(block_of, first, step_size, 0)
        targets = lax.dynamic_slice_in_dim(target_ids, first, step_size, 0)
        live = lax.dynamic_slice_in_dim(live_slot, first, step_size, 0)
        one_hot = (blocks[:, None] == source_ids[None, :]).astype(jnp.bfloat16)
        picked = jnp.einsum(
            "tk,kif->tif", one_hot, table_blocks, preferred_element_type=jnp.float32
        ).astype(jnp.bfloat16)
        products = jnp.einsum("tij,tjf->tif", tiles, picked, preferred_element_type=jnp.float32)
        selector = ((targets[None, :] == dest_ids[:, None]) & live[None, :]).astype(jnp.float32)
        return totals + jnp.einsum(
            "qt,tif->qif", selector, products, precision=lax.Precision.HIGHEST
        )

    empty = jnp.zeros((dest_blocks, tile_width, feat_width), jnp.float32)
    return lax.fori_loop(0, rounds, one_round, empty)


def per_device(features, edge_tiles, tile_src, tile_dst, tile_count, weight, out_bias):
    tiles_here = edge_tiles[0, 0]
    source_ids = tile_src[0, 0]
    target_ids = tile_dst[0, 0]
    live_count = tile_count[0, 0]
    slot_total = tiles_here.shape[0]
    tile_width = tiles_here.shape[-1]
    node_rows = features.shape[0]
    feat_width = features.shape[1]
    group_count = lax.axis_size("row")
    dest_blocks = group_count * node_rows // tile_width
    slot_ids = jnp.arange(slot_total, dtype=jnp.int32)
    live_slot = slot_ids < live_count
    table = lax.all_gather(features, "blk", axis=0, tiled=True)
    totals = accumulate(table, source_ids, tiles_here, target_ids, live_slot, dest_blocks).reshape(
        -1, feat_width
    )
    row_sums = jnp.sum(tiles_here, axis=2, dtype=jnp.float32)
    block_ids = jnp.arange(dest_blocks, dtype=jnp.int32)
    selector = ((target_ids[None, :] == block_ids[:, None]) & live_slot[None, :]).astype(
        jnp.float32
    )
    degree_part = jnp.dot(selector, row_sums, precision=lax.Precision.HIGHEST).reshape(-1)
    aggregate, degree = (
        lax.psum_scatter(
            totals.astype(jnp.bfloat16), "row", scatter_dimension=0, tiled=True
        ).astype(jnp.float32),
        lax.psum_scatter(
            degree_part.astype(jnp.bfloat16), "row", scatter_dimension=0, tiled=True
        ).astype(jnp.float32),
    )
    neighbor_mean = (aggregate / jnp.maximum(degree, 1.0)[:, None]).astype(jnp.bfloat16)
    joined = jnp.concatenate([features, neighbor_mean], axis=1)
    mixed = jnp.dot(joined, weight, preferred_element_type=jnp.float32) + out_bias
    return jax.nn.relu(mixed).astype(jnp.bfloat16)


def solution(mesh):
    in_specs = (
        P(("row", "blk"), None),
        P("row", "blk", None, None, None),
        P("row", "blk", None),
        P("row", "blk", None),
        P("row", "blk"),
        P(),
        P(),
    )
    out_specs = P(("row", "blk"), None)

    def body(features, edge_tiles, *rest):
        dense = 2 * lax.axis_size("row") * lax.axis_size("blk") * features.shape[0] ** 2
        run = per_device_fused if dense <= DENSE_LIMIT else per_device
        return run(features, edge_tiles, *rest)

    return jax.shard_map(
        body, mesh=mesh, in_specs=in_specs, out_specs=out_specs, check_vma=False
    )
```

```python
import functools

import jax
import jax.numpy as jnp
from jax import lax
from jax.experimental import pallas as pl
from jax.experimental.pallas import tpu as pltpu
from jax.sharding import PartitionSpec as P

MESH = pl.DeviceIdType.MESH
CHUNK = 128
AHEAD = 2
DENSE_LIMIT = 12 * 2**20


def fused(
    rows_n, spots, live_hbm, src_hbm, dst_hbm, feat_hbm, tiles_hbm, weight_hbm, bias_hbm, out_ref,
    live_ref, src_ref, dst_ref, bias_ref, tab, tiles, chain, dense, weight, mine, acc, mixed, degree, send_buf, recv_buf, lists, list_smem,
    in_sem, own_sem, left_sem, right_sem, far_left_sem, far_right_sem, side_sem, line_recv, side_recv, row_send, row_recv,
):
    slots = tiles.shape[0]
    width = tiles.shape[-1]
    chunks = tab.shape[0]
    node_rows = mine.shape[0]
    feat = mine.shape[1]
    per_node = node_rows // width
    sources = spots * 2 * per_node
    dests = rows_n * per_node
    wide = 2 * per_node
    row = lax.axis_index("row")
    blk = lax.axis_index("blk")
    z = blk // 2
    c = blk % 2
    side = z * 2 + (1 - c)

    barrier = pltpu.get_barrier_semaphore()

    def greet(r, b):
        pl.semaphore_signal(barrier, inc=1, device_id=(r, b), device_id_type=MESH)

    @pl.when(z > 0)
    def _():
        greet(row, blk - 2)

    @pl.when(z < spots - 1)
    def _():
        greet(row, blk + 2)

    @pl.when(z > 1)
    def _():
        greet(row, blk - 4)

    @pl.when(z < spots - 2)
    def _():
        greet(row, blk + 4)

    greet(row, side)
    for step in range(1, rows_n):
        greet((row + step) % rows_n, blk)

    def own_local(k):
        return pltpu.make_async_copy(
            feat_hbm.at[:, pl.ds(pl.multiple_of(k * CHUNK, CHUNK), CHUNK)], tab.at[k, z, c], own_sem.at[k]
        )

    def line_copy(k, p, step, sems):
        slot = tab.at[k, p, c]
        return pltpu.make_async_remote_copy(
            src_ref=slot, dst_ref=slot, send_sem=sems.at[k, p], recv_sem=line_recv.at[k, p],
            device_id=(row, blk + 2 * step), device_id_type=MESH,
        )

    def far_copy(k, step, sems):
        slot = tab.at[k, z, c]
        return pltpu.make_async_remote_copy(
            src_ref=slot, dst_ref=slot, send_sem=sems.at[k], recv_sem=line_recv.at[k, z],
            device_id=(row, blk + 4 * step), device_id_type=MESH,
        )

    def side_copy(k, p):
        slot = tab.at[k, p, c]
        return pltpu.make_async_remote_copy(
            src_ref=slot, dst_ref=slot, send_sem=side_sem.at[k, p], recv_sem=side_recv.at[k, p],
            device_id=(row, side), device_id_type=MESH,
        )

    def side_arrival(k, p):
        slot = tab.at[k, p, 1 - c]
        return pltpu.make_async_remote_copy(
            src_ref=slot, dst_ref=slot, send_sem=side_sem.at[k, p], recv_sem=side_recv.at[k, p],
            device_id=(row, side), device_id_type=MESH,
        )

    def row_copy(k, step):
        peer = (row + step) % rows_n
        return pltpu.make_async_remote_copy(
            src_ref=send_buf.at[k, peer], dst_ref=recv_buf.at[k, row],
            send_sem=row_send.at[k, peer], recv_sem=row_recv.at[k, row],
            device_id=(peer, blk), device_id_type=MESH,
        )

    def row_arrival(k, step):
        peer = (row + step) % rows_n
        return pltpu.make_async_remote_copy(
            src_ref=send_buf.at[k, peer], dst_ref=recv_buf.at[k, peer],
            send_sem=row_send.at[k, peer], recv_sem=row_recv.at[k, peer],
            device_id=(peer, blk), device_id_type=MESH,
        )

    def send_own(k):
        own_local(k).wait()

        @pl.when(z > 0)
        def _():
            line_copy(k, z, -1, left_sem).start()

        @pl.when(z < spots - 1)
        def _():
            line_copy(k, z, 1, right_sem).start()

        @pl.when(z > 1)
        def _():
            far_copy(k, -1, far_left_sem).start()

        @pl.when(z < spots - 2)
        def _():
            far_copy(k, 1, far_right_sem).start()

        side_copy(k, z).start()

    loads = [
        pltpu.make_async_copy(tiles_hbm, tiles, in_sem.at[0]),
        pltpu.make_async_copy(feat_hbm, mine, in_sem.at[1]),
        pltpu.make_async_copy(weight_hbm, weight, in_sem.at[2]),
        pltpu.make_async_copy(bias_hbm, bias_ref, in_sem.at[4]),
        pltpu.make_async_copy(live_hbm, live_ref, in_sem.at[5]),
        pltpu.make_async_copy(src_hbm, src_ref, in_sem.at[6]),
        pltpu.make_async_copy(dst_hbm, dst_ref, in_sem.at[7]),
    ]
    for load in loads[4:]:
        load.start()
    for k in range(chunks):
        own_local(k).start()
    loads[0].start()

    greeted = (
        jnp.where(z > 0, 1, 0) + jnp.where(z < spots - 1, 1, 0) + rows_n
        + jnp.where(z > 1, 1, 0) + jnp.where(z < spots - 2, 1, 0)
    )
    pl.semaphore_wait(barrier, greeted)

    def first_sends(k, carry):
        send_own(k)
        return carry

    lax.fori_loop(0, min(AHEAD, chunks), first_sends, 0)
    for load in loads[1:4]:
        load.start()
    for load in loads[4:]:
        load.wait()

    list_rows = lists.shape[0] - 1
    lane = lax.broadcasted_iota(jnp.int32, (1, 128), 1)
    place = lax.broadcasted_iota(jnp.int32, (list_rows, 128), 0) * 128 + lax.broadcasted_iota(
        jnp.int32, (list_rows, 128), 1
    )
    live = live_ref[0, 0]

    def one_key(t, carry):
        keys, last = carry
        key = dst_ref[0, 0, t] * sources + src_ref[0, 0, t]
        key = jnp.where(t < live, key, -1)
        return jnp.where(lane == t, key, keys), jnp.where(place == key, t, last)

    keys, last = lax.fori_loop(
        0, slots, one_key,
        (jnp.full((1, 128), -1, jnp.int32), jnp.full((list_rows, 128), slots, jnp.int32)), unroll=8,
    )

    def one_before(u, before):
        key = dst_ref[0, 0, u] * sources + src_ref[0, 0, u]
        key = jnp.where(u < live, key, -2)
        return jnp.where((keys == key) & (lane > u), u, before)

    before = lax.fori_loop(0, slots, one_before, jnp.full((1, 128), slots, jnp.int32), unroll=8)
    lists[pl.ds(0, list_rows), :] = last
    lists[pl.ds(list_rows, 1), :] = before
    to_smem = pltpu.make_async_copy(lists, list_smem, in_sem.at[3])
    to_smem.start()
    chain[slots] = jnp.zeros((width, width), jnp.float32)
    loads[0].wait()
    to_smem.wait()

    def one_link(t, carry):
        chain[t] = tiles[t].astype(jnp.float32) + chain[list_smem[list_rows, t]]
        return carry

    lax.fori_loop(0, slots, one_link, 0, unroll=4)

    def one_dest(q, carry):
        total = jnp.zeros((width, width), jnp.float32)
        for s in range(sources):
            at = q * sources + s
            block = chain[list_smem[at // 128, at % 128]]
            dense[s // wide, pl.ds(pl.multiple_of(q * width, width), width), pl.ds(s % wide * width, width)] = (
                block.astype(jnp.bfloat16)
            )
            total += block
        degrees = jnp.broadcast_to(jnp.sum(total, axis=1, keepdims=True), (width, CHUNK))
        send_buf[chunks, q // per_node, pl.ds(pl.multiple_of(q % per_node * width, width), width), :] = (
            degrees.astype(jnp.bfloat16)
        )
        return carry

    lax.fori_loop(0, dests, one_dest, 0)


    def consume(k, p, first):
        block = tab[k, p].reshape(wide * width, CHUNK)
        product = jnp.dot(dense[p], block, preferred_element_type=jnp.float32)
        if first:
            acc[k] = product
        else:
            acc[k] += product

    def send_rows(k):
        for step in range(1, rows_n):
            row_copy(k, step).start()

    def gather_rows(k):
        total = send_buf[k, row].astype(jnp.float32)
        for step in range(1, rows_n):
            row_arrival(k, step).wait_recv()
            total += recv_buf[k, (row + step) % rows_n].astype(jnp.float32)
        return total

    def forward(k, h):
        @pl.when(z + h < spots)
        def _():
            line_copy(k, z + h, -1, left_sem).wait_recv()
            if h > 1:

                @pl.when(z > 0)
                def _():
                    line_copy(k, z + h, -1, left_sem).start()

            side_copy(k, z + h).start()

        @pl.when(z - h >= 0)
        def _():
            line_copy(k, z - h, 1, right_sem).wait_recv()
            if h > 1:

                @pl.when(z < spots - 1)
                def _():
                    line_copy(k, z - h, 1, right_sem).start()

            side_copy(k, z - h).start()

    def consume_at(k, h):
        if h == 0:
            side_arrival(k, z).wait_recv()
            consume(k, z, True)
            return

        @pl.when(z + h < spots)
        def _():
            side_arrival(k, z + h).wait_recv()
            consume(k, z + h, False)

        @pl.when(z - h >= 0)
        def _():
            side_arrival(k, z - h).wait_recv()
            consume(k, z - h, False)

    def finish_mean(k):
        mean = (gather_rows(k) / degree[...]).astype(jnp.bfloat16)
        part = weight[pl.ds(pl.multiple_of(feat + k * CHUNK, CHUNK), CHUNK), :]
        mixed[...] += jnp.dot(mean, part, preferred_element_type=jnp.float32)

    send_rows(chunks)

    def stage(k, carry):
        for h in range(1, min(3, spots)):
            forward(k, h)

        @pl.when(k + AHEAD < chunks)
        def _():
            send_own(k + AHEAD)

        for h in range(spots):
            if h > 2:
                forward(k, h)
            consume_at(k, h)
        send_buf[k] = acc[k].astype(jnp.bfloat16).reshape(rows_n, node_rows, CHUNK)
        send_rows(k)

        @pl.when(k == 0)
        def _():
            for load in loads[1:4]:
                load.wait()
            mixed[...] = (
                jnp.dot(mine[...], weight[pl.ds(0, feat), :], preferred_element_type=jnp.float32) + bias_ref[...]
            )
            degree[...] = jnp.maximum(gather_rows(chunks), 1.0)

        @pl.when(k > 0)
        def _():
            finish_mean(k - 1)

        return carry

    lax.fori_loop(0, chunks, stage, 0)
    finish_mean(chunks - 1)
    out_ref[...] = jnp.maximum(mixed[...], 0.0).astype(jnp.bfloat16)

    def finish(k, carry):
        side_copy(k, z).wait_send()

        @pl.when(z > 0)
        def _():
            line_copy(k, z, -1, left_sem).wait_send()

        @pl.when(z < spots - 1)
        def _():
            line_copy(k, z, 1, right_sem).wait_send()

        @pl.when(z > 1)
        def _():
            far_copy(k, -1, far_left_sem).wait_send()

        @pl.when(z < spots - 2)
        def _():
            far_copy(k, 1, far_right_sem).wait_send()

        for h in range(1, spots):

            @pl.when(z + h < spots)
            def _():
                side_copy(k, z + h).wait_send()
                if h > 1:

                    @pl.when(z > 0)
                    def _():
                        line_copy(k, z + h, -1, left_sem).wait_send()

            @pl.when(z - h >= 0)
            def _():
                side_copy(k, z - h).wait_send()
                if h > 1:

                    @pl.when(z < spots - 1)
                    def _():
                        line_copy(k, z - h, 1, right_sem).wait_send()

        return carry

    lax.fori_loop(0, chunks, finish, 0)

    def finish_rows(k, carry):
        for step in range(1, rows_n):
            row_copy(k, step).wait_send()
        return carry

    lax.fori_loop(0, chunks + 1, finish_rows, 0)


def per_device_fused(features, edge_tiles, tile_src, tile_dst, tile_count, weight, out_bias):
    rows_n = lax.axis_size("row")
    spots = lax.axis_size("blk") // 2
    slots, width = edge_tiles.shape[2], edge_tiles.shape[-1]
    node_rows, feat = features.shape
    chunks = feat // CHUNK
    per_node = node_rows // width
    dests, sources = rows_n * per_node, spots * 2 * per_node
    list_rows = -(-dests * sources // 128)
    dest_rows = rows_n * node_rows
    hbm = pl.BlockSpec(memory_space=pltpu.HBM)
    vmem = pl.BlockSpec(memory_space=pltpu.VMEM)
    dma = pltpu.SemaphoreType.DMA
    return pl.pallas_call(
        functools.partial(fused, rows_n, spots),
        out_shape=jax.ShapeDtypeStruct((node_rows, feat), jnp.bfloat16),
        in_specs=[hbm] * 7,
        out_specs=vmem,
        scratch_shapes=[
            pltpu.SMEM(tile_count.shape, jnp.int32),
            pltpu.SMEM(tile_src.shape, jnp.int32),
            pltpu.SMEM(tile_dst.shape, jnp.int32),
            pltpu.VMEM((1, feat), jnp.float32),
            pltpu.VMEM((chunks, spots, 2, node_rows, CHUNK), jnp.bfloat16),
            pltpu.VMEM((slots, width, width), jnp.bfloat16),
            pltpu.VMEM((slots + 1, width, width), jnp.float32),
            pltpu.VMEM((spots, dest_rows, 2 * node_rows), jnp.bfloat16),
            pltpu.VMEM(weight.shape, jnp.bfloat16),
            pltpu.VMEM((node_rows, feat), jnp.bfloat16),
            pltpu.VMEM((chunks, dest_rows, CHUNK), jnp.float32),
            pltpu.VMEM((node_rows, feat), jnp.float32),
            pltpu.VMEM((node_rows, CHUNK), jnp.float32),
            pltpu.VMEM((chunks + 1, rows_n, node_rows, CHUNK), jnp.bfloat16),
            pltpu.VMEM((chunks + 1, rows_n, node_rows, CHUNK), jnp.bfloat16),
            pltpu.VMEM((list_rows + 1, 128), jnp.int32),
            pltpu.SMEM((list_rows + 1, 128), jnp.int32),
            dma((8,)),
            dma((chunks,)),
            dma((chunks, spots)),
            dma((chunks, spots)),
            dma((chunks,)),
            dma((chunks,)),
            dma((chunks, spots)),
            dma((chunks, spots)),
            dma((chunks, spots)),
            dma((chunks + 1, rows_n)),
            dma((chunks + 1, rows_n)),
        ],
        compiler_params=pltpu.CompilerParams(
            collective_id=0, has_side_effects=True, vmem_limit_bytes=56 * 2**20
        ),
    )(
        tile_count,
        tile_src,
        tile_dst,
        features,
        edge_tiles.reshape(slots, width, width),
        weight,
        out_bias.reshape(1, feat),
    )


def accumulate(table, block_of, tiles_here, target_ids, live_slot, dest_blocks):
    slot_total = tiles_here.shape[0]
    tile_width = tiles_here.shape[-1]
    feat_width = table.shape[1]
    table_blocks = table.reshape(-1, tile_width, feat_width)
    source_total = table_blocks.shape[0]
    step_size = 16
    rounds = slot_total // step_size
    source_ids = jnp.arange(source_total, dtype=jnp.int32)
    dest_ids = jnp.arange(dest_blocks, dtype=jnp.int32)

    def one_round(index, totals):
        first = index * step_size
        tiles = lax.dynamic_slice_in_dim(tiles_here, first, step_size, 0)
        blocks = lax.dynamic_slice_in_dim(block_of, first, step_size, 0)
        targets = lax.dynamic_slice_in_dim(target_ids, first, step_size, 0)
        live = lax.dynamic_slice_in_dim(live_slot, first, step_size, 0)
        one_hot = (blocks[:, None] == source_ids[None, :]).astype(jnp.bfloat16)
        picked = jnp.einsum(
            "tk,kif->tif", one_hot, table_blocks, preferred_element_type=jnp.float32
        ).astype(jnp.bfloat16)
        products = jnp.einsum("tij,tjf->tif", tiles, picked, preferred_element_type=jnp.float32)
        selector = ((targets[None, :] == dest_ids[:, None]) & live[None, :]).astype(jnp.float32)
        return totals + jnp.einsum(
            "qt,tif->qif", selector, products, precision=lax.Precision.HIGHEST
        )

    empty = jnp.zeros((dest_blocks, tile_width, feat_width), jnp.float32)
    return lax.fori_loop(0, rounds, one_round, empty)


def per_device(features, edge_tiles, tile_src, tile_dst, tile_count, weight, out_bias):
    tiles_here = edge_tiles[0, 0]
    source_ids = tile_src[0, 0]
    target_ids = tile_dst[0, 0]
    live_count = tile_count[0, 0]
    slot_total = tiles_here.shape[0]
    tile_width = tiles_here.shape[-1]
    node_rows = features.shape[0]
    feat_width = features.shape[1]
    group_count = lax.axis_size("row")
    dest_blocks = group_count * node_rows // tile_width
    slot_ids = jnp.arange(slot_total, dtype=jnp.int32)
    live_slot = slot_ids < live_count
    table = lax.all_gather(features, "blk", axis=0, tiled=True)
    totals = accumulate(table, source_ids, tiles_here, target_ids, live_slot, dest_blocks).reshape(
        -1, feat_width
    )
    row_sums = jnp.sum(tiles_here, axis=2, dtype=jnp.float32)
    block_ids = jnp.arange(dest_blocks, dtype=jnp.int32)
    selector = ((target_ids[None, :] == block_ids[:, None]) & live_slot[None, :]).astype(
        jnp.float32
    )
    degree_part = jnp.dot(selector, row_sums, precision=lax.Precision.HIGHEST).reshape(-1)
    aggregate, degree = (
        lax.psum_scatter(
            totals.astype(jnp.bfloat16), "row", scatter_dimension=0, tiled=True
        ).astype(jnp.float32),
        lax.psum_scatter(
            degree_part.astype(jnp.bfloat16), "row", scatter_dimension=0, tiled=True
        ).astype(jnp.float32),
    )
    neighbor_mean = (aggregate / jnp.maximum(degree, 1.0)[:, None]).astype(jnp.bfloat16)
    joined = jnp.concatenate([features, neighbor_mean], axis=1)
    mixed = jnp.dot(joined, weight, preferred_element_type=jnp.float32) + out_bias
    return jax.nn.relu(mixed).astype(jnp.bfloat16)


def solution(mesh):
    in_specs = (
        P(("row", "blk"), None),
        P("row", "blk", None, None, None),
        P("row", "blk", None),
        P("row", "blk", None),
        P("row", "blk"),
        P(),
        P(),
    )
    out_specs = P(("row", "blk"), None)

    def body(features, edge_tiles, *rest):
        dense = 2 * lax.axis_size("row") * lax.axis_size("blk") * features.shape[0] ** 2
        run = per_device_fused if dense <= DENSE_LIMIT else per_device
        return run(features, edge_tiles, *rest)

    return jax.shard_map(
        body, mesh=mesh, in_specs=in_specs, out_specs=out_specs, check_vma=False
    )
```

```python
import functools

import jax
import jax.numpy as jnp
from jax import lax
from jax.experimental import pallas as pl
from jax.experimental.pallas import tpu as pltpu
from jax.sharding import PartitionSpec as P

MESH = pl.DeviceIdType.MESH
CHUNK = 128
AHEAD = 2
FAR = 2
DENSE_LIMIT = 12 * 2**20


def fused(
    rows_n, spots, live_hbm, src_hbm, dst_hbm, feat_hbm, tiles_hbm, weight_hbm, bias_hbm, out_ref,
    live_ref, src_ref, dst_ref, bias_ref, tab, tiles, chain, dense, weight, mine, acc, mixed, degree, send_buf, recv_buf, lists, list_smem,
    in_sem, own_sem, left_sem, right_sem, far_left_sem, far_right_sem, side_sem, line_recv, side_recv, row_send, row_recv,
):
    slots = tiles.shape[0]
    width = tiles.shape[-1]
    chunks = tab.shape[0]
    node_rows = mine.shape[0]
    feat = mine.shape[1]
    per_node = node_rows // width
    sources = spots * 2 * per_node
    dests = rows_n * per_node
    wide = 2 * per_node
    row = lax.axis_index("row")
    blk = lax.axis_index("blk")
    z = blk // 2
    c = blk % 2
    side = z * 2 + (1 - c)

    barrier = pltpu.get_barrier_semaphore()

    def greet(r, b):
        pl.semaphore_signal(barrier, inc=1, device_id=(r, b), device_id_type=MESH)

    @pl.when(z > 0)
    def _():
        greet(row, blk - 2)

    @pl.when(z < spots - 1)
    def _():
        greet(row, blk + 2)

    @pl.when(z > 1)
    def _():
        greet(row, blk - 4)

    @pl.when(z < spots - 2)
    def _():
        greet(row, blk + 4)

    greet(row, side)
    for step in range(1, rows_n):
        greet((row + step) % rows_n, blk)

    def own_local(k):
        return pltpu.make_async_copy(
            feat_hbm.at[:, pl.ds(pl.multiple_of(k * CHUNK, CHUNK), CHUNK)], tab.at[k, z, c], own_sem.at[k]
        )

    def line_copy(k, p, step, sems):
        slot = tab.at[k, p, c]
        return pltpu.make_async_remote_copy(
            src_ref=slot, dst_ref=slot, send_sem=sems.at[k, p], recv_sem=line_recv.at[k, p],
            device_id=(row, blk + 2 * step), device_id_type=MESH,
        )

    def far_copy(k, step, sems):
        slot = tab.at[k, z, c]
        return pltpu.make_async_remote_copy(
            src_ref=slot, dst_ref=slot, send_sem=sems.at[k], recv_sem=line_recv.at[k, z],
            device_id=(row, blk + 4 * step), device_id_type=MESH,
        )

    def side_copy(k, p):
        slot = tab.at[k, p, c]
        return pltpu.make_async_remote_copy(
            src_ref=slot, dst_ref=slot, send_sem=side_sem.at[k, p], recv_sem=side_recv.at[k, p],
            device_id=(row, side), device_id_type=MESH,
        )

    def side_arrival(k, p):
        slot = tab.at[k, p, 1 - c]
        return pltpu.make_async_remote_copy(
            src_ref=slot, dst_ref=slot, send_sem=side_sem.at[k, p], recv_sem=side_recv.at[k, p],
            device_id=(row, side), device_id_type=MESH,
        )

    def row_copy(k, step):
        peer = (row + step) % rows_n
        return pltpu.make_async_remote_copy(
            src_ref=send_buf.at[k, peer], dst_ref=recv_buf.at[k, row],
            send_sem=row_send.at[k, peer], recv_sem=row_recv.at[k, row],
            device_id=(peer, blk), device_id_type=MESH,
        )

    def row_arrival(k, step):
        peer = (row + step) % rows_n
        return pltpu.make_async_remote_copy(
            src_ref=send_buf.at[k, peer], dst_ref=recv_buf.at[k, peer],
            send_sem=row_send.at[k, peer], recv_sem=row_recv.at[k, peer],
            device_id=(peer, blk), device_id_type=MESH,
        )

    def send_own(k):
        own_local(k).wait()

        @pl.when(z > 0)
        def _():
            line_copy(k, z, -1, left_sem).start()

        @pl.when(z < spots - 1)
        def _():
            line_copy(k, z, 1, right_sem).start()

        @pl.when((z > 1) & (k < FAR))
        def _():
            far_copy(k, -1, far_left_sem).start()

        @pl.when((z < spots - 2) & (k < FAR))
        def _():
            far_copy(k, 1, far_right_sem).start()

        side_copy(k, z).start()

    loads = [
        pltpu.make_async_copy(tiles_hbm, tiles, in_sem.at[0]),
        pltpu.make_async_copy(feat_hbm, mine, in_sem.at[1]),
        pltpu.make_async_copy(weight_hbm, weight, in_sem.at[2]),
        pltpu.make_async_copy(bias_hbm, bias_ref, in_sem.at[4]),
        pltpu.make_async_copy(live_hbm, live_ref, in_sem.at[5]),
        pltpu.make_async_copy(src_hbm, src_ref, in_sem.at[6]),
        pltpu.make_async_copy(dst_hbm, dst_ref, in_sem.at[7]),
    ]
    for load in loads[4:]:
        load.start()
    for k in range(chunks):
        own_local(k).start()
    loads[0].start()

    greeted = (
        jnp.where(z > 0, 1, 0) + jnp.where(z < spots - 1, 1, 0) + rows_n
        + jnp.where(z > 1, 1, 0) + jnp.where(z < spots - 2, 1, 0)
    )
    pl.semaphore_wait(barrier, greeted)

    def first_sends(k, carry):
        send_own(k)
        return carry

    lax.fori_loop(0, min(AHEAD, chunks), first_sends, 0)
    for load in loads[1:4]:
        load.start()
    for load in loads[4:]:
        load.wait()

    list_rows = lists.shape[0] - 1
    lane = lax.broadcasted_iota(jnp.int32, (1, 128), 1)
    place = lax.broadcasted_iota(jnp.int32, (list_rows, 128), 0) * 128 + lax.broadcasted_iota(
        jnp.int32, (list_rows, 128), 1
    )
    live = live_ref[0, 0]

    def one_key(t, carry):
        keys, last = carry
        key = dst_ref[0, 0, t] * sources + src_ref[0, 0, t]
        key = jnp.where(t < live, key, -1)
        return jnp.where(lane == t, key, keys), jnp.where(place == key, t, last)

    keys, last = lax.fori_loop(
        0, slots, one_key,
        (jnp.full((1, 128), -1, jnp.int32), jnp.full((list_rows, 128), slots, jnp.int32)), unroll=8,
    )

    def one_before(u, before):
        key = dst_ref[0, 0, u] * sources + src_ref[0, 0, u]
        key = jnp.where(u < live, key, -2)
        return jnp.where((keys == key) & (lane > u), u, before)

    before = lax.fori_loop(0, slots, one_before, jnp.full((1, 128), slots, jnp.int32), unroll=8)
    lists[pl.ds(0, list_rows), :] = last
    lists[pl.ds(list_rows, 1), :] = before
    to_smem = pltpu.make_async_copy(lists, list_smem, in_sem.at[3])
    to_smem.start()
    chain[slots] = jnp.zeros((width, width), jnp.float32)
    loads[0].wait()
    to_smem.wait()

    def one_link(t, carry):
        chain[t] = tiles[t].astype(jnp.float32) + chain[list_smem[list_rows, t]]
        return carry

    lax.fori_loop(0, slots, one_link, 0, unroll=4)

    def one_dest(q, carry):
        total = jnp.zeros((width, width), jnp.float32)
        for s in range(sources):
            at = q * sources + s
            block = chain[list_smem[at // 128, at % 128]]
            dense[s // wide, pl.ds(pl.multiple_of(q * width, width), width), pl.ds(s % wide * width, width)] = (
                block.astype(jnp.bfloat16)
            )
            total += block
        degrees = jnp.broadcast_to(jnp.sum(total, axis=1, keepdims=True), (width, CHUNK))
        send_buf[chunks, q // per_node, pl.ds(pl.multiple_of(q % per_node * width, width), width), :] = (
            degrees.astype(jnp.bfloat16)
        )
        return carry

    lax.fori_loop(0, dests, one_dest, 0)


    def consume(k, p, first):
        block = tab[k, p].reshape(wide * width, CHUNK)
        product = jnp.dot(dense[p], block, preferred_element_type=jnp.float32)
        if first:
            acc[k] = product
        else:
            acc[k] += product

    def send_rows(k):
        for step in range(1, rows_n):
            row_copy(k, step).start()

    def gather_rows(k):
        total = send_buf[k, row].astype(jnp.float32)
        for step in range(1, rows_n):
            row_arrival(k, step).wait_recv()
            total += recv_buf[k, (row + step) % rows_n].astype(jnp.float32)
        return total

    def handed(k, h):
        return (k >= FAR) | (h > 1)

    def forward(k, h):
        @pl.when(z + h < spots)
        def _():
            line_copy(k, z + h, -1, left_sem).wait_recv()

            @pl.when((z > 0) & handed(k, h))
            def _():
                line_copy(k, z + h, -1, left_sem).start()

            side_copy(k, z + h).start()

        @pl.when(z - h >= 0)
        def _():
            line_copy(k, z - h, 1, right_sem).wait_recv()

            @pl.when((z < spots - 1) & handed(k, h))
            def _():
                line_copy(k, z - h, 1, right_sem).start()

            side_copy(k, z - h).start()

    def consume_at(k, h):
        if h == 0:
            side_arrival(k, z).wait_recv()
            consume(k, z, True)
            return

        @pl.when(z + h < spots)
        def _():
            side_arrival(k, z + h).wait_recv()
            consume(k, z + h, False)

        @pl.when(z - h >= 0)
        def _():
            side_arrival(k, z - h).wait_recv()
            consume(k, z - h, False)

    def finish_mean(k):
        mean = (gather_rows(k) / degree[...]).astype(jnp.bfloat16)
        part = weight[pl.ds(pl.multiple_of(feat + k * CHUNK, CHUNK), CHUNK), :]
        mixed[...] += jnp.dot(mean, part, preferred_element_type=jnp.float32)

    send_rows(chunks)
    inner = (z > 0) & (z < spots - 1)

    def pass_on(k):
        forward(k, 1)

        @pl.when(k + AHEAD < chunks)
        def _():
            send_own(k + AHEAD)

        for h in range(2, min(3, spots)):
            forward(k, h)

    pass_on(0)

    def stage(k, carry):
        @pl.when(inner & (k + 1 < chunks))
        def _():
            pass_on(k + 1)

        for h in range(spots):
            if h > 2:
                forward(k, h)
            consume_at(k, h)
        send_buf[k] = acc[k].astype(jnp.bfloat16).reshape(rows_n, node_rows, CHUNK)
        send_rows(k)

        @pl.when(jnp.logical_not(inner) & (k + 1 < chunks))
        def _():
            pass_on(k + 1)

        @pl.when(k == 0)
        def _():
            for load in loads[1:4]:
                load.wait()
            mixed[...] = (
                jnp.dot(mine[...], weight[pl.ds(0, feat), :], preferred_element_type=jnp.float32) + bias_ref[...]
            )
            degree[...] = jnp.maximum(gather_rows(chunks), 1.0)

        @pl.when(k > 0)
        def _():
            finish_mean(k - 1)

        return carry

    lax.fori_loop(0, chunks, stage, 0)
    finish_mean(chunks - 1)
    out_ref[...] = mixed[...].astype(jnp.bfloat16)

    def finish(k, carry):
        side_copy(k, z).wait_send()

        @pl.when(z > 0)
        def _():
            line_copy(k, z, -1, left_sem).wait_send()

        @pl.when(z < spots - 1)
        def _():
            line_copy(k, z, 1, right_sem).wait_send()

        @pl.when((z > 1) & (k < FAR))
        def _():
            far_copy(k, -1, far_left_sem).wait_send()

        @pl.when((z < spots - 2) & (k < FAR))
        def _():
            far_copy(k, 1, far_right_sem).wait_send()

        for h in range(1, spots):

            @pl.when(z + h < spots)
            def _():
                side_copy(k, z + h).wait_send()

                @pl.when((z > 0) & handed(k, h))
                def _():
                    line_copy(k, z + h, -1, left_sem).wait_send()

            @pl.when(z - h >= 0)
            def _():
                side_copy(k, z - h).wait_send()

                @pl.when((z < spots - 1) & handed(k, h))
                def _():
                    line_copy(k, z - h, 1, right_sem).wait_send()

        return carry

    lax.fori_loop(0, chunks, finish, 0)

    def finish_rows(k, carry):
        for step in range(1, rows_n):
            row_copy(k, step).wait_send()
        return carry

    lax.fori_loop(0, chunks + 1, finish_rows, 0)


def per_device_fused(features, edge_tiles, tile_src, tile_dst, tile_count, weight, out_bias):
    rows_n = lax.axis_size("row")
    spots = lax.axis_size("blk") // 2
    slots, width = edge_tiles.shape[2], edge_tiles.shape[-1]
    node_rows, feat = features.shape
    chunks = feat // CHUNK
    per_node = node_rows // width
    dests, sources = rows_n * per_node, spots * 2 * per_node
    list_rows = -(-dests * sources // 128)
    dest_rows = rows_n * node_rows
    hbm = pl.BlockSpec(memory_space=pltpu.HBM)
    vmem = pl.BlockSpec(memory_space=pltpu.VMEM)
    dma = pltpu.SemaphoreType.DMA
    mixed = pl.pallas_call(
        functools.partial(fused, rows_n, spots),
        out_shape=jax.ShapeDtypeStruct((node_rows, feat), jnp.bfloat16),
        in_specs=[hbm] * 7,
        out_specs=vmem,
        scratch_shapes=[
            pltpu.SMEM(tile_count.shape, jnp.int32),
            pltpu.SMEM(tile_src.shape, jnp.int32),
            pltpu.SMEM(tile_dst.shape, jnp.int32),
            pltpu.VMEM((1, feat), jnp.float32),
            pltpu.VMEM((chunks, spots, 2, node_rows, CHUNK), jnp.bfloat16),
            pltpu.VMEM((slots, width, width), jnp.bfloat16),
            pltpu.VMEM((slots + 1, width, width), jnp.float32),
            pltpu.VMEM((spots, dest_rows, 2 * node_rows), jnp.bfloat16),
            pltpu.VMEM(weight.shape, jnp.bfloat16),
            pltpu.VMEM((node_rows, feat), jnp.bfloat16),
            pltpu.VMEM((chunks, dest_rows, CHUNK), jnp.float32),
            pltpu.VMEM((node_rows, feat), jnp.float32),
            pltpu.VMEM((node_rows, CHUNK), jnp.float32),
            pltpu.VMEM((chunks + 1, rows_n, node_rows, CHUNK), jnp.bfloat16),
            pltpu.VMEM((chunks + 1, rows_n, node_rows, CHUNK), jnp.bfloat16),
            pltpu.VMEM((list_rows + 1, 128), jnp.int32),
            pltpu.SMEM((list_rows + 1, 128), jnp.int32),
            dma((8,)),
            dma((chunks,)),
            dma((chunks, spots)),
            dma((chunks, spots)),
            dma((chunks,)),
            dma((chunks,)),
            dma((chunks, spots)),
            dma((chunks, spots)),
            dma((chunks, spots)),
            dma((chunks + 1, rows_n)),
            dma((chunks + 1, rows_n)),
        ],
        compiler_params=pltpu.CompilerParams(
            collective_id=0, has_side_effects=True, vmem_limit_bytes=56 * 2**20
        ),
    )(
        tile_count,
        tile_src,
        tile_dst,
        features,
        edge_tiles.reshape(slots, width, width),
        weight,
        out_bias.reshape(1, feat),
    )
    return jax.nn.relu(mixed)


def accumulate(table, block_of, tiles_here, target_ids, live_slot, dest_blocks):
    slot_total = tiles_here.shape[0]
    tile_width = tiles_here.shape[-1]
    feat_width = table.shape[1]
    table_blocks = table.reshape(-1, tile_width, feat_width)
    source_total = table_blocks.shape[0]
    step_size = 16
    rounds = slot_total // step_size
    source_ids = jnp.arange(source_total, dtype=jnp.int32)
    dest_ids = jnp.arange(dest_blocks, dtype=jnp.int32)

    def one_round(index, totals):
        first = index * step_size
        tiles = lax.dynamic_slice_in_dim(tiles_here, first, step_size, 0)
        blocks = lax.dynamic_slice_in_dim(block_of, first, step_size, 0)
        targets = lax.dynamic_slice_in_dim(target_ids, first, step_size, 0)
        live = lax.dynamic_slice_in_dim(live_slot, first, step_size, 0)
        one_hot = (blocks[:, None] == source_ids[None, :]).astype(jnp.bfloat16)
        picked = jnp.einsum(
            "tk,kif->tif", one_hot, table_blocks, preferred_element_type=jnp.float32
        ).astype(jnp.bfloat16)
        products = jnp.einsum("tij,tjf->tif", tiles, picked, preferred_element_type=jnp.float32)
        selector = ((targets[None, :] == dest_ids[:, None]) & live[None, :]).astype(jnp.float32)
        return totals + jnp.einsum(
            "qt,tif->qif", selector, products, precision=lax.Precision.HIGHEST
        )

    empty = jnp.zeros((dest_blocks, tile_width, feat_width), jnp.float32)
    return lax.fori_loop(0, rounds, one_round, empty)


def per_device(features, edge_tiles, tile_src, tile_dst, tile_count, weight, out_bias):
    tiles_here = edge_tiles[0, 0]
    source_ids = tile_src[0, 0]
    target_ids = tile_dst[0, 0]
    live_count = tile_count[0, 0]
    slot_total = tiles_here.shape[0]
    tile_width = tiles_here.shape[-1]
    node_rows = features.shape[0]
    feat_width = features.shape[1]
    group_count = lax.axis_size("row")
    dest_blocks = group_count * node_rows // tile_width
    slot_ids = jnp.arange(slot_total, dtype=jnp.int32)
    live_slot = slot_ids < live_count
    table = lax.all_gather(features, "blk", axis=0, tiled=True)
    totals = accumulate(table, source_ids, tiles_here, target_ids, live_slot, dest_blocks).reshape(
        -1, feat_width
    )
    row_sums = jnp.sum(tiles_here, axis=2, dtype=jnp.float32)
    block_ids = jnp.arange(dest_blocks, dtype=jnp.int32)
    selector = ((target_ids[None, :] == block_ids[:, None]) & live_slot[None, :]).astype(
        jnp.float32
    )
    degree_part = jnp.dot(selector, row_sums, precision=lax.Precision.HIGHEST).reshape(-1)
    aggregate, degree = (
        lax.psum_scatter(
            totals.astype(jnp.bfloat16), "row", scatter_dimension=0, tiled=True
        ).astype(jnp.float32),
        lax.psum_scatter(
            degree_part.astype(jnp.bfloat16), "row", scatter_dimension=0, tiled=True
        ).astype(jnp.float32),
    )
    neighbor_mean = (aggregate / jnp.maximum(degree, 1.0)[:, None]).astype(jnp.bfloat16)
    joined = jnp.concatenate([features, neighbor_mean], axis=1)
    mixed = jnp.dot(joined, weight, preferred_element_type=jnp.float32) + out_bias
    return jax.nn.relu(mixed).astype(jnp.bfloat16)


def solution(mesh):
    in_specs = (
        P(("row", "blk"), None),
        P("row", "blk", None, None, None),
        P("row", "blk", None),
        P("row", "blk", None),
        P("row", "blk"),
        P(),
        P(),
    )
    out_specs = P(("row", "blk"), None)

    def body(features, edge_tiles, *rest):
        dense = 2 * lax.axis_size("row") * lax.axis_size("blk") * features.shape[0] ** 2
        run = per_device_fused if dense <= DENSE_LIMIT else per_device
        return run(features, edge_tiles, *rest)

    return jax.shard_map(
        body, mesh=mesh, in_specs=in_specs, out_specs=out_specs, check_vma=False
    )
```

```python
import functools

import jax
import jax.numpy as jnp
from jax import lax
from jax.experimental import pallas as pl
from jax.experimental.pallas import tpu as pltpu
from jax.sharding import PartitionSpec as P

MESH = pl.DeviceIdType.MESH
CHUNK = 128
AHEAD = 3
FAR = 4
DENSE_LIMIT = 12 * 2**20


def fused(
    rows_n, spots, live_hbm, src_hbm, dst_hbm, feat_hbm, tiles_hbm, weight_hbm, bias_hbm, out_ref,
    live_ref, src_ref, dst_ref, bias_ref, tab, tiles, chain, dense, weight, mine, acc, mixed, degree, send_buf, recv_buf, lists, list_smem,
    in_sem, own_sem, left_sem, right_sem, far_left_sem, far_right_sem, side_sem, line_recv, side_recv, row_send, row_recv,
):
    slots = tiles.shape[0]
    width = tiles.shape[-1]
    chunks = tab.shape[0]
    node_rows = mine.shape[0]
    feat = mine.shape[1]
    per_node = node_rows // width
    sources = spots * 2 * per_node
    dests = rows_n * per_node
    wide = 2 * per_node
    row = lax.axis_index("row")
    blk = lax.axis_index("blk")
    z = blk // 2
    c = blk % 2
    side = z * 2 + (1 - c)

    barrier = pltpu.get_barrier_semaphore()

    def greet(r, b):
        pl.semaphore_signal(barrier, inc=1, device_id=(r, b), device_id_type=MESH)

    @pl.when(z > 0)
    def _():
        greet(row, blk - 2)

    @pl.when(z < spots - 1)
    def _():
        greet(row, blk + 2)

    @pl.when(z > 1)
    def _():
        greet(row, blk - 4)

    @pl.when(z < spots - 2)
    def _():
        greet(row, blk + 4)

    greet(row, side)
    for step in range(1, rows_n):
        greet((row + step) % rows_n, blk)

    def own_local(k):
        return pltpu.make_async_copy(
            feat_hbm.at[:, pl.ds(pl.multiple_of(k * CHUNK, CHUNK), CHUNK)], tab.at[k, z, c], own_sem.at[k]
        )

    def line_copy(k, p, step, sems):
        slot = tab.at[k, p, c]
        return pltpu.make_async_remote_copy(
            src_ref=slot, dst_ref=slot, send_sem=sems.at[k, p], recv_sem=line_recv.at[k, p],
            device_id=(row, blk + 2 * step), device_id_type=MESH,
        )

    def far_copy(k, step, sems):
        slot = tab.at[k, z, c]
        return pltpu.make_async_remote_copy(
            src_ref=slot, dst_ref=slot, send_sem=sems.at[k], recv_sem=line_recv.at[k, z],
            device_id=(row, blk + 4 * step), device_id_type=MESH,
        )

    def side_copy(k, p):
        slot = tab.at[k, p, c]
        return pltpu.make_async_remote_copy(
            src_ref=slot, dst_ref=slot, send_sem=side_sem.at[k, p], recv_sem=side_recv.at[k, p],
            device_id=(row, side), device_id_type=MESH,
        )

    def side_arrival(k, p):
        slot = tab.at[k, p, 1 - c]
        return pltpu.make_async_remote_copy(
            src_ref=slot, dst_ref=slot, send_sem=side_sem.at[k, p], recv_sem=side_recv.at[k, p],
            device_id=(row, side), device_id_type=MESH,
        )

    def row_copy(k, step):
        peer = (row + step) % rows_n
        return pltpu.make_async_remote_copy(
            src_ref=send_buf.at[k, peer], dst_ref=recv_buf.at[k, row],
            send_sem=row_send.at[k, peer], recv_sem=row_recv.at[k, row],
            device_id=(peer, blk), device_id_type=MESH,
        )

    def row_arrival(k, step):
        peer = (row + step) % rows_n
        return pltpu.make_async_remote_copy(
            src_ref=send_buf.at[k, peer], dst_ref=recv_buf.at[k, peer],
            send_sem=row_send.at[k, peer], recv_sem=row_recv.at[k, peer],
            device_id=(peer, blk), device_id_type=MESH,
        )

    def send_own(k):
        own_local(k).wait()

        @pl.when(z > 0)
        def _():
            line_copy(k, z, -1, left_sem).start()

        @pl.when(z < spots - 1)
        def _():
            line_copy(k, z, 1, right_sem).start()

        @pl.when((z > 1) & (k < FAR))
        def _():
            far_copy(k, -1, far_left_sem).start()

        @pl.when((z < spots - 2) & (k < FAR))
        def _():
            far_copy(k, 1, far_right_sem).start()

        side_copy(k, z).start()

    loads = [
        pltpu.make_async_copy(tiles_hbm, tiles, in_sem.at[0]),
        pltpu.make_async_copy(feat_hbm, mine, in_sem.at[1]),
        pltpu.make_async_copy(weight_hbm, weight, in_sem.at[2]),
        pltpu.make_async_copy(bias_hbm, bias_ref, in_sem.at[4]),
        pltpu.make_async_copy(live_hbm, live_ref, in_sem.at[5]),
        pltpu.make_async_copy(src_hbm, src_ref, in_sem.at[6]),
        pltpu.make_async_copy(dst_hbm, dst_ref, in_sem.at[7]),
    ]
    for load in loads[4:]:
        load.start()
    for k in range(chunks):
        own_local(k).start()
    loads[0].start()

    greeted = (
        jnp.where(z > 0, 1, 0) + jnp.where(z < spots - 1, 1, 0) + rows_n
        + jnp.where(z > 1, 1, 0) + jnp.where(z < spots - 2, 1, 0)
    )
    pl.semaphore_wait(barrier, greeted)

    def first_sends(k, carry):
        send_own(k)
        return carry

    lax.fori_loop(0, min(AHEAD, chunks), first_sends, 0)
    for load in loads[1:4]:
        load.start()
    for load in loads[4:]:
        load.wait()

    list_rows = lists.shape[0] - 1
    lane = lax.broadcasted_iota(jnp.int32, (1, 128), 1)
    place = lax.broadcasted_iota(jnp.int32, (list_rows, 128), 0) * 128 + lax.broadcasted_iota(
        jnp.int32, (list_rows, 128), 1
    )
    live = live_ref[0, 0]

    def one_key(t, carry):
        keys, last = carry
        key = dst_ref[0, 0, t] * sources + src_ref[0, 0, t]
        key = jnp.where(t < live, key, -1)
        return jnp.where(lane == t, key, keys), jnp.where(place == key, t, last)

    keys, last = lax.fori_loop(
        0, slots, one_key,
        (jnp.full((1, 128), -1, jnp.int32), jnp.full((list_rows, 128), slots, jnp.int32)), unroll=8,
    )

    def one_before(u, before):
        key = dst_ref[0, 0, u] * sources + src_ref[0, 0, u]
        key = jnp.where(u < live, key, -2)
        return jnp.where((keys == key) & (lane > u), u, before)

    before = lax.fori_loop(0, slots, one_before, jnp.full((1, 128), slots, jnp.int32), unroll=8)
    lists[pl.ds(0, list_rows), :] = last
    lists[pl.ds(list_rows, 1), :] = before
    to_smem = pltpu.make_async_copy(lists, list_smem, in_sem.at[3])
    to_smem.start()
    chain[slots] = jnp.zeros((width, width), jnp.float32)
    loads[0].wait()
    to_smem.wait()

    def one_link(t, carry):
        chain[t] = tiles[t].astype(jnp.float32) + chain[list_smem[list_rows, t]]
        return carry

    lax.fori_loop(0, slots, one_link, 0, unroll=4)

    def one_dest(q, carry):
        total = jnp.zeros((width, width), jnp.float32)
        for s in range(sources):
            at = q * sources + s
            block = chain[list_smem[at // 128, at % 128]]
            dense[s // wide, pl.ds(pl.multiple_of(q * width, width), width), pl.ds(s % wide * width, width)] = (
                block.astype(jnp.bfloat16)
            )
            total += block
        degrees = jnp.broadcast_to(jnp.sum(total, axis=1, keepdims=True), (width, CHUNK))
        send_buf[chunks, q // per_node, pl.ds(pl.multiple_of(q % per_node * width, width), width), :] = (
            degrees.astype(jnp.bfloat16)
        )
        return carry


    def consume(k, p, first):
        block = tab[k, p].reshape(wide * width, CHUNK)
        product = jnp.dot(dense[p], block, preferred_element_type=jnp.float32)
        if first:
            acc[k] = product
        else:
            acc[k] += product

    def send_rows(k):
        for step in range(1, rows_n):
            row_copy(k, step).start()

    def gather_rows(k):
        total = send_buf[k, row].astype(jnp.float32)
        for step in range(1, rows_n):
            row_arrival(k, step).wait_recv()
            total += recv_buf[k, (row + step) % rows_n].astype(jnp.float32)
        return total

    def handed(k, h):
        return (k >= FAR) | (h > 1)

    def forward(k, h):
        @pl.when(z + h < spots)
        def _():
            line_copy(k, z + h, -1, left_sem).wait_recv()

            @pl.when((z > 0) & handed(k, h))
            def _():
                line_copy(k, z + h, -1, left_sem).start()

            side_copy(k, z + h).start()

        @pl.when(z - h >= 0)
        def _():
            line_copy(k, z - h, 1, right_sem).wait_recv()

            @pl.when((z < spots - 1) & handed(k, h))
            def _():
                line_copy(k, z - h, 1, right_sem).start()

            side_copy(k, z - h).start()

    def near(k):
        forward(k, 1)

        @pl.when(k + AHEAD < chunks)
        def _():
            send_own(k + AHEAD)

    def far(k):
        if spots > 2:
            forward(k, 2)

    def consume_at(k, h):
        if h == 0:
            side_arrival(k, z).wait_recv()
            consume(k, z, True)
            return

        @pl.when(z + h < spots)
        def _():
            side_arrival(k, z + h).wait_recv()
            consume(k, z + h, False)

        @pl.when(z - h >= 0)
        def _():
            side_arrival(k, z - h).wait_recv()
            consume(k, z - h, False)

    def finish_mean(k):
        mean = (gather_rows(k) / degree[...]).astype(jnp.bfloat16)
        part = weight[pl.ds(pl.multiple_of(feat + k * CHUNK, CHUNK), CHUNK), :]
        mixed[...] += jnp.dot(mean, part, preferred_element_type=jnp.float32)

    near(0)
    lax.fori_loop(0, dests, one_dest, 0)
    send_rows(chunks)
    def stage(k, carry):
        @pl.when(k > 0)
        def _():
            near(k)

        far(k)
        for h in range(spots):
            if h > 2:
                forward(k, h)
            consume_at(k, h)
        send_buf[k] = acc[k].astype(jnp.bfloat16).reshape(rows_n, node_rows, CHUNK)
        send_rows(k)

        @pl.when(k == 0)
        def _():
            for load in loads[1:4]:
                load.wait()
            mixed[...] = (
                jnp.dot(mine[...], weight[pl.ds(0, feat), :], preferred_element_type=jnp.float32) + bias_ref[...]
            )
            degree[...] = jnp.maximum(gather_rows(chunks), 1.0)

        @pl.when(k > 0)
        def _():
            finish_mean(k - 1)

        return carry

    lax.fori_loop(0, chunks, stage, 0)
    finish_mean(chunks - 1)
    out_ref[...] = mixed[...].astype(jnp.bfloat16)

    def finish(k, carry):
        side_copy(k, z).wait_send()

        @pl.when(z > 0)
        def _():
            line_copy(k, z, -1, left_sem).wait_send()

        @pl.when(z < spots - 1)
        def _():
            line_copy(k, z, 1, right_sem).wait_send()

        @pl.when((z > 1) & (k < FAR))
        def _():
            far_copy(k, -1, far_left_sem).wait_send()

        @pl.when((z < spots - 2) & (k < FAR))
        def _():
            far_copy(k, 1, far_right_sem).wait_send()

        for h in range(1, spots):

            @pl.when(z + h < spots)
            def _():
                side_copy(k, z + h).wait_send()

                @pl.when((z > 0) & handed(k, h))
                def _():
                    line_copy(k, z + h, -1, left_sem).wait_send()

            @pl.when(z - h >= 0)
            def _():
                side_copy(k, z - h).wait_send()

                @pl.when((z < spots - 1) & handed(k, h))
                def _():
                    line_copy(k, z - h, 1, right_sem).wait_send()

        return carry

    lax.fori_loop(0, chunks, finish, 0)

    def finish_rows(k, carry):
        for step in range(1, rows_n):
            row_copy(k, step).wait_send()
        return carry

    lax.fori_loop(0, chunks + 1, finish_rows, 0)


def per_device_fused(features, edge_tiles, tile_src, tile_dst, tile_count, weight, out_bias):
    rows_n = lax.axis_size("row")
    spots = lax.axis_size("blk") // 2
    slots, width = edge_tiles.shape[2], edge_tiles.shape[-1]
    node_rows, feat = features.shape
    chunks = feat // CHUNK
    per_node = node_rows // width
    dests, sources = rows_n * per_node, spots * 2 * per_node
    list_rows = -(-dests * sources // 128)
    dest_rows = rows_n * node_rows
    hbm = pl.BlockSpec(memory_space=pltpu.HBM)
    vmem = pl.BlockSpec(memory_space=pltpu.VMEM)
    dma = pltpu.SemaphoreType.DMA
    mixed = pl.pallas_call(
        functools.partial(fused, rows_n, spots),
        out_shape=jax.ShapeDtypeStruct((node_rows, feat), jnp.bfloat16),
        in_specs=[hbm] * 7,
        out_specs=vmem,
        scratch_shapes=[
            pltpu.SMEM(tile_count.shape, jnp.int32),
            pltpu.SMEM(tile_src.shape, jnp.int32),
            pltpu.SMEM(tile_dst.shape, jnp.int32),
            pltpu.VMEM((1, feat), jnp.float32),
            pltpu.VMEM((chunks, spots, 2, node_rows, CHUNK), jnp.bfloat16),
            pltpu.VMEM((slots, width, width), jnp.bfloat16),
            pltpu.VMEM((slots + 1, width, width), jnp.float32),
            pltpu.VMEM((spots, dest_rows, 2 * node_rows), jnp.bfloat16),
            pltpu.VMEM(weight.shape, jnp.bfloat16),
            pltpu.VMEM((node_rows, feat), jnp.bfloat16),
            pltpu.VMEM((chunks, dest_rows, CHUNK), jnp.float32),
            pltpu.VMEM((node_rows, feat), jnp.float32),
            pltpu.VMEM((node_rows, CHUNK), jnp.float32),
            pltpu.VMEM((chunks + 1, rows_n, node_rows, CHUNK), jnp.bfloat16),
            pltpu.VMEM((chunks + 1, rows_n, node_rows, CHUNK), jnp.bfloat16),
            pltpu.VMEM((list_rows + 1, 128), jnp.int32),
            pltpu.SMEM((list_rows + 1, 128), jnp.int32),
            dma((8,)),
            dma((chunks,)),
            dma((chunks, spots)),
            dma((chunks, spots)),
            dma((chunks,)),
            dma((chunks,)),
            dma((chunks, spots)),
            dma((chunks, spots)),
            dma((chunks, spots)),
            dma((chunks + 1, rows_n)),
            dma((chunks + 1, rows_n)),
        ],
        compiler_params=pltpu.CompilerParams(
            collective_id=0, has_side_effects=True, vmem_limit_bytes=56 * 2**20
        ),
    )(
        tile_count,
        tile_src,
        tile_dst,
        features,
        edge_tiles.reshape(slots, width, width),
        weight,
        out_bias.reshape(1, feat),
    )
    return jax.nn.relu(mixed)


def accumulate(table, block_of, tiles_here, target_ids, live_slot, dest_blocks):
    slot_total = tiles_here.shape[0]
    tile_width = tiles_here.shape[-1]
    feat_width = table.shape[1]
    table_blocks = table.reshape(-1, tile_width, feat_width)
    source_total = table_blocks.shape[0]
    step_size = 16
    rounds = slot_total // step_size
    source_ids = jnp.arange(source_total, dtype=jnp.int32)
    dest_ids = jnp.arange(dest_blocks, dtype=jnp.int32)

    def one_round(index, totals):
        first = index * step_size
        tiles = lax.dynamic_slice_in_dim(tiles_here, first, step_size, 0)
        blocks = lax.dynamic_slice_in_dim(block_of, first, step_size, 0)
        targets = lax.dynamic_slice_in_dim(target_ids, first, step_size, 0)
        live = lax.dynamic_slice_in_dim(live_slot, first, step_size, 0)
        one_hot = (blocks[:, None] == source_ids[None, :]).astype(jnp.bfloat16)
        picked = jnp.einsum(
            "tk,kif->tif", one_hot, table_blocks, preferred_element_type=jnp.float32
        ).astype(jnp.bfloat16)
        products = jnp.einsum("tij,tjf->tif", tiles, picked, preferred_element_type=jnp.float32)
        selector = ((targets[None, :] == dest_ids[:, None]) & live[None, :]).astype(jnp.float32)
        return totals + jnp.einsum(
            "qt,tif->qif", selector, products, precision=lax.Precision.HIGHEST
        )

    empty = jnp.zeros((dest_blocks, tile_width, feat_width), jnp.float32)
    return lax.fori_loop(0, rounds, one_round, empty)


def per_device(features, edge_tiles, tile_src, tile_dst, tile_count, weight, out_bias):
    tiles_here = edge_tiles[0, 0]
    source_ids = tile_src[0, 0]
    target_ids = tile_dst[0, 0]
    live_count = tile_count[0, 0]
    slot_total = tiles_here.shape[0]
    tile_width = tiles_here.shape[-1]
    node_rows = features.shape[0]
    feat_width = features.shape[1]
    group_count = lax.axis_size("row")
    dest_blocks = group_count * node_rows // tile_width
    slot_ids = jnp.arange(slot_total, dtype=jnp.int32)
    live_slot = slot_ids < live_count
    table = lax.all_gather(features, "blk", axis=0, tiled=True)
    totals = accumulate(table, source_ids, tiles_here, target_ids, live_slot, dest_blocks).reshape(
        -1, feat_width
    )
    row_sums = jnp.sum(tiles_here, axis=2, dtype=jnp.float32)
    block_ids = jnp.arange(dest_blocks, dtype=jnp.int32)
    selector = ((target_ids[None, :] == block_ids[:, None]) & live_slot[None, :]).astype(
        jnp.float32
    )
    degree_part = jnp.dot(selector, row_sums, precision=lax.Precision.HIGHEST).reshape(-1)
    aggregate, degree = (
        lax.psum_scatter(
            totals.astype(jnp.bfloat16), "row", scatter_dimension=0, tiled=True
        ).astype(jnp.float32),
        lax.psum_scatter(
            degree_part.astype(jnp.bfloat16), "row", scatter_dimension=0, tiled=True
        ).astype(jnp.float32),
    )
    neighbor_mean = (aggregate / jnp.maximum(degree, 1.0)[:, None]).astype(jnp.bfloat16)
    joined = jnp.concatenate([features, neighbor_mean], axis=1)
    mixed = jnp.dot(joined, weight, preferred_element_type=jnp.float32) + out_bias
    return jax.nn.relu(mixed).astype(jnp.bfloat16)


def solution(mesh):
    in_specs = (
        P(("row", "blk"), None),
        P("row", "blk", None, None, None),
        P("row", "blk", None),
        P("row", "blk", None),
        P("row", "blk"),
        P(),
        P(),
    )
    out_specs = P(("row", "blk"), None)

    def body(features, edge_tiles, *rest):
        dense = 2 * lax.axis_size("row") * lax.axis_size("blk") * features.shape[0] ** 2
        run = per_device_fused if dense <= DENSE_LIMIT else per_device
        return run(features, edge_tiles, *rest)

    return jax.shard_map(
        body, mesh=mesh, in_specs=in_specs, out_specs=out_specs, check_vma=False
    )
```

```python
import functools

import jax
import jax.numpy as jnp
from jax import lax
from jax.experimental import pallas as pl
from jax.experimental.pallas import tpu as pltpu
from jax.sharding import PartitionSpec as P

MESH = pl.DeviceIdType.MESH
CHUNK = 256
AHEAD = 2
DENSE_LIMIT = 12 * 2**20


def fused(
    rows_n, spots, live_hbm, src_hbm, dst_hbm, feat_hbm, tiles_hbm, weight_hbm, bias_hbm, out_ref,
    live_ref, src_ref, dst_ref, bias_ref, tab, tiles, chain, dense, weight, mine, acc, mixed, degree, send_buf, recv_buf, lists, list_smem,
    in_sem, own_sem, left_sem, right_sem, far_left_sem, far_right_sem, side_sem, line_recv, side_recv, row_send, row_recv,
):
    slots = tiles.shape[0]
    width = tiles.shape[-1]
    chunks = tab.shape[0]
    node_rows = mine.shape[0]
    feat = mine.shape[1]
    per_node = node_rows // width
    sources = spots * 2 * per_node
    dests = rows_n * per_node
    wide = 2 * per_node
    row = lax.axis_index("row")
    blk = lax.axis_index("blk")
    z = blk // 2
    c = blk % 2
    side = z * 2 + (1 - c)

    barrier = pltpu.get_barrier_semaphore()

    def greet(r, b):
        pl.semaphore_signal(barrier, inc=1, device_id=(r, b), device_id_type=MESH)

    @pl.when(z > 0)
    def _():
        greet(row, blk - 2)

    @pl.when(z < spots - 1)
    def _():
        greet(row, blk + 2)

    @pl.when(z > 1)
    def _():
        greet(row, blk - 4)

    @pl.when(z < spots - 2)
    def _():
        greet(row, blk + 4)

    greet(row, side)
    for step in range(1, rows_n):
        greet((row + step) % rows_n, blk)

    def own_local(k):
        return pltpu.make_async_copy(
            feat_hbm.at[:, pl.ds(pl.multiple_of(k * CHUNK, CHUNK), CHUNK)], tab.at[k, z, c], own_sem.at[k]
        )

    def line_copy(k, p, step, sems):
        slot = tab.at[k, p, c]
        return pltpu.make_async_remote_copy(
            src_ref=slot, dst_ref=slot, send_sem=sems.at[k, p], recv_sem=line_recv.at[k, p],
            device_id=(row, blk + 2 * step), device_id_type=MESH,
        )

    def far_copy(k, step, sems):
        slot = tab.at[k, z, c]
        return pltpu.make_async_remote_copy(
            src_ref=slot, dst_ref=slot, send_sem=sems.at[k], recv_sem=line_recv.at[k, z],
            device_id=(row, blk + 4 * step), device_id_type=MESH,
        )

    def side_copy(k, p):
        slot = tab.at[k, p, c]
        return pltpu.make_async_remote_copy(
            src_ref=slot, dst_ref=slot, send_sem=side_sem.at[k, p], recv_sem=side_recv.at[k, p],
            device_id=(row, side), device_id_type=MESH,
        )

    def side_arrival(k, p):
        slot = tab.at[k, p, 1 - c]
        return pltpu.make_async_remote_copy(
            src_ref=slot, dst_ref=slot, send_sem=side_sem.at[k, p], recv_sem=side_recv.at[k, p],
            device_id=(row, side), device_id_type=MESH,
        )

    def row_copy(k, step):
        peer = (row + step) % rows_n
        return pltpu.make_async_remote_copy(
            src_ref=send_buf.at[k, peer], dst_ref=recv_buf.at[k, row],
            send_sem=row_send.at[k, peer], recv_sem=row_recv.at[k, row],
            device_id=(peer, blk), device_id_type=MESH,
        )

    def row_arrival(k, step):
        peer = (row + step) % rows_n
        return pltpu.make_async_remote_copy(
            src_ref=send_buf.at[k, peer], dst_ref=recv_buf.at[k, peer],
            send_sem=row_send.at[k, peer], recv_sem=row_recv.at[k, peer],
            device_id=(peer, blk), device_id_type=MESH,
        )

    def send_own(k):
        own_local(k).wait()

        @pl.when(z > 0)
        def _():
            line_copy(k, z, -1, left_sem).start()

        @pl.when(z < spots - 1)
        def _():
            line_copy(k, z, 1, right_sem).start()

        @pl.when(z > 1)
        def _():
            far_copy(k, -1, far_left_sem).start()

        @pl.when(z < spots - 2)
        def _():
            far_copy(k, 1, far_right_sem).start()

        side_copy(k, z).start()

    loads = [
        pltpu.make_async_copy(tiles_hbm, tiles, in_sem.at[0]),
        pltpu.make_async_copy(feat_hbm, mine, in_sem.at[1]),
        pltpu.make_async_copy(weight_hbm, weight, in_sem.at[2]),
        pltpu.make_async_copy(bias_hbm, bias_ref, in_sem.at[4]),
        pltpu.make_async_copy(live_hbm, live_ref, in_sem.at[5]),
        pltpu.make_async_copy(src_hbm, src_ref, in_sem.at[6]),
        pltpu.make_async_copy(dst_hbm, dst_ref, in_sem.at[7]),
    ]
    for load in loads[4:]:
        load.start()
    for k in range(chunks):
        own_local(k).start()
    loads[0].start()

    greeted = (
        jnp.where(z > 0, 1, 0) + jnp.where(z < spots - 1, 1, 0) + rows_n
        + jnp.where(z > 1, 1, 0) + jnp.where(z < spots - 2, 1, 0)
    )
    pl.semaphore_wait(barrier, greeted)

    def first_sends(k, carry):
        send_own(k)
        return carry

    lax.fori_loop(0, min(AHEAD, chunks), first_sends, 0)
    for load in loads[1:4]:
        load.start()
    for load in loads[4:]:
        load.wait()

    list_rows = lists.shape[0] - 1
    lane = lax.broadcasted_iota(jnp.int32, (1, 128), 1)
    place = lax.broadcasted_iota(jnp.int32, (list_rows, 128), 0) * 128 + lax.broadcasted_iota(
        jnp.int32, (list_rows, 128), 1
    )
    live = live_ref[0, 0]

    def one_key(t, carry):
        keys, last = carry
        key = dst_ref[0, 0, t] * sources + src_ref[0, 0, t]
        key = jnp.where(t < live, key, -1)
        return jnp.where(lane == t, key, keys), jnp.where(place == key, t, last)

    keys, last = lax.fori_loop(
        0, slots, one_key,
        (jnp.full((1, 128), -1, jnp.int32), jnp.full((list_rows, 128), slots, jnp.int32)), unroll=8,
    )

    def one_before(u, before):
        key = dst_ref[0, 0, u] * sources + src_ref[0, 0, u]
        key = jnp.where(u < live, key, -2)
        return jnp.where((keys == key) & (lane > u), u, before)

    before = lax.fori_loop(0, slots, one_before, jnp.full((1, 128), slots, jnp.int32), unroll=8)
    lists[pl.ds(0, list_rows), :] = last
    lists[pl.ds(list_rows, 1), :] = before
    to_smem = pltpu.make_async_copy(lists, list_smem, in_sem.at[3])
    to_smem.start()
    chain[slots] = jnp.zeros((width, width), jnp.float32)
    loads[0].wait()
    to_smem.wait()

    def one_link(t, carry):
        chain[t] = tiles[t].astype(jnp.float32) + chain[list_smem[list_rows, t]]
        return carry

    lax.fori_loop(0, slots, one_link, 0, unroll=4)

    def one_dest(q, carry):
        total = jnp.zeros((width, width), jnp.float32)
        for s in range(sources):
            at = q * sources + s
            block = chain[list_smem[at // 128, at % 128]]
            dense[s // wide, pl.ds(pl.multiple_of(q * width, width), width), pl.ds(s % wide * width, width)] = (
                block.astype(jnp.bfloat16)
            )
            total += block
        degrees = jnp.broadcast_to(jnp.sum(total, axis=1, keepdims=True), (width, CHUNK))
        send_buf[chunks, q // per_node, pl.ds(pl.multiple_of(q % per_node * width, width), width), :] = (
            degrees.astype(jnp.bfloat16)
        )
        return carry

    lax.fori_loop(0, dests, one_dest, 0)


    def consume(k, p, first):
        block = tab[k, p].reshape(wide * width, CHUNK)
        product = jnp.dot(dense[p], block, preferred_element_type=jnp.float32)
        if first:
            acc[k] = product
        else:
            acc[k] += product

    def send_rows(k):
        for step in range(1, rows_n):
            row_copy(k, step).start()

    def gather_rows(k):
        total = send_buf[k, row].astype(jnp.float32)
        for step in range(1, rows_n):
            row_arrival(k, step).wait_recv()
            total += recv_buf[k, (row + step) % rows_n].astype(jnp.float32)
        return total

    def forward(k, h):
        @pl.when(z + h < spots)
        def _():
            line_copy(k, z + h, -1, left_sem).wait_recv()
            if h > 1:

                @pl.when(z > 0)
                def _():
                    line_copy(k, z + h, -1, left_sem).start()

            side_copy(k, z + h).start()

        @pl.when(z - h >= 0)
        def _():
            line_copy(k, z - h, 1, right_sem).wait_recv()
            if h > 1:

                @pl.when(z < spots - 1)
                def _():
                    line_copy(k, z - h, 1, right_sem).start()

            side_copy(k, z - h).start()

    def consume_at(k, h):
        if h == 0:
            side_arrival(k, z).wait_recv()
            consume(k, z, True)
            return

        @pl.when(z + h < spots)
        def _():
            side_arrival(k, z + h).wait_recv()
            consume(k, z + h, False)

        @pl.when(z - h >= 0)
        def _():
            side_arrival(k, z - h).wait_recv()
            consume(k, z - h, False)

    def finish_mean(k):
        mean = (gather_rows(k) / degree[...]).astype(jnp.bfloat16)
        part = weight[pl.ds(pl.multiple_of(feat + k * CHUNK, CHUNK), CHUNK), :]
        mixed[...] += jnp.dot(mean, part, preferred_element_type=jnp.float32)

    send_rows(chunks)

    def stage(k, carry):
        for h in range(1, min(3, spots)):
            forward(k, h)

        @pl.when(k + AHEAD < chunks)
        def _():
            send_own(k + AHEAD)

        for h in range(spots):
            if h > 2:
                forward(k, h)
            consume_at(k, h)
        send_buf[k] = acc[k].astype(jnp.bfloat16).reshape(rows_n, node_rows, CHUNK)
        send_rows(k)

        @pl.when(k == 0)
        def _():
            for load in loads[1:4]:
                load.wait()
            mixed[...] = (
                jnp.dot(mine[...], weight[pl.ds(0, feat), :], preferred_element_type=jnp.float32) + bias_ref[...]
            )
            degree[...] = jnp.maximum(gather_rows(chunks), 1.0)

        @pl.when(k > 0)
        def _():
            finish_mean(k - 1)

        return carry

    lax.fori_loop(0, chunks, stage, 0)
    finish_mean(chunks - 1)
    out_ref[...] = jnp.maximum(mixed[...], 0.0).astype(jnp.bfloat16)

    def finish(k, carry):
        side_copy(k, z).wait_send()

        @pl.when(z > 0)
        def _():
            line_copy(k, z, -1, left_sem).wait_send()

        @pl.when(z < spots - 1)
        def _():
            line_copy(k, z, 1, right_sem).wait_send()

        @pl.when(z > 1)
        def _():
            far_copy(k, -1, far_left_sem).wait_send()

        @pl.when(z < spots - 2)
        def _():
            far_copy(k, 1, far_right_sem).wait_send()

        for h in range(1, spots):

            @pl.when(z + h < spots)
            def _():
                side_copy(k, z + h).wait_send()
                if h > 1:

                    @pl.when(z > 0)
                    def _():
                        line_copy(k, z + h, -1, left_sem).wait_send()

            @pl.when(z - h >= 0)
            def _():
                side_copy(k, z - h).wait_send()
                if h > 1:

                    @pl.when(z < spots - 1)
                    def _():
                        line_copy(k, z - h, 1, right_sem).wait_send()

        return carry

    lax.fori_loop(0, chunks, finish, 0)

    def finish_rows(k, carry):
        for step in range(1, rows_n):
            row_copy(k, step).wait_send()
        return carry

    lax.fori_loop(0, chunks + 1, finish_rows, 0)


def per_device_fused(features, edge_tiles, tile_src, tile_dst, tile_count, weight, out_bias):
    rows_n = lax.axis_size("row")
    spots = lax.axis_size("blk") // 2
    slots, width = edge_tiles.shape[2], edge_tiles.shape[-1]
    node_rows, feat = features.shape
    chunks = feat // CHUNK
    per_node = node_rows // width
    dests, sources = rows_n * per_node, spots * 2 * per_node
    list_rows = -(-dests * sources // 128)
    dest_rows = rows_n * node_rows
    hbm = pl.BlockSpec(memory_space=pltpu.HBM)
    vmem = pl.BlockSpec(memory_space=pltpu.VMEM)
    dma = pltpu.SemaphoreType.DMA
    return pl.pallas_call(
        functools.partial(fused, rows_n, spots),
        out_shape=jax.ShapeDtypeStruct((node_rows, feat), jnp.bfloat16),
        in_specs=[hbm] * 7,
        out_specs=vmem,
        scratch_shapes=[
            pltpu.SMEM(tile_count.shape, jnp.int32),
            pltpu.SMEM(tile_src.shape, jnp.int32),
            pltpu.SMEM(tile_dst.shape, jnp.int32),
            pltpu.VMEM((1, feat), jnp.float32),
            pltpu.VMEM((chunks, spots, 2, node_rows, CHUNK), jnp.bfloat16),
            pltpu.VMEM((slots, width, width), jnp.bfloat16),
            pltpu.VMEM((slots + 1, width, width), jnp.float32),
            pltpu.VMEM((spots, dest_rows, 2 * node_rows), jnp.bfloat16),
            pltpu.VMEM(weight.shape, jnp.bfloat16),
            pltpu.VMEM((node_rows, feat), jnp.bfloat16),
            pltpu.VMEM((chunks, dest_rows, CHUNK), jnp.float32),
            pltpu.VMEM((node_rows, feat), jnp.float32),
            pltpu.VMEM((node_rows, CHUNK), jnp.float32),
            pltpu.VMEM((chunks + 1, rows_n, node_rows, CHUNK), jnp.bfloat16),
            pltpu.VMEM((chunks + 1, rows_n, node_rows, CHUNK), jnp.bfloat16),
            pltpu.VMEM((list_rows + 1, 128), jnp.int32),
            pltpu.SMEM((list_rows + 1, 128), jnp.int32),
            dma((8,)),
            dma((chunks,)),
            dma((chunks, spots)),
            dma((chunks, spots)),
            dma((chunks,)),
            dma((chunks,)),
            dma((chunks, spots)),
            dma((chunks, spots)),
            dma((chunks, spots)),
            dma((chunks + 1, rows_n)),
            dma((chunks + 1, rows_n)),
        ],
        compiler_params=pltpu.CompilerParams(
            collective_id=0, has_side_effects=True, vmem_limit_bytes=56 * 2**20
        ),
    )(
        tile_count,
        tile_src,
        tile_dst,
        features,
        edge_tiles.reshape(slots, width, width),
        weight,
        out_bias.reshape(1, feat),
    )


def accumulate(table, block_of, tiles_here, target_ids, live_slot, dest_blocks):
    slot_total = tiles_here.shape[0]
    tile_width = tiles_here.shape[-1]
    feat_width = table.shape[1]
    table_blocks = table.reshape(-1, tile_width, feat_width)
    source_total = table_blocks.shape[0]
    step_size = 16
    rounds = slot_total // step_size
    source_ids = jnp.arange(source_total, dtype=jnp.int32)
    dest_ids = jnp.arange(dest_blocks, dtype=jnp.int32)

    def one_round(index, totals):
        first = index * step_size
        tiles = lax.dynamic_slice_in_dim(tiles_here, first, step_size, 0)
        blocks = lax.dynamic_slice_in_dim(block_of, first, step_size, 0)
        targets = lax.dynamic_slice_in_dim(target_ids, first, step_size, 0)
        live = lax.dynamic_slice_in_dim(live_slot, first, step_size, 0)
        one_hot = (blocks[:, None] == source_ids[None, :]).astype(jnp.bfloat16)
        picked = jnp.einsum(
            "tk,kif->tif", one_hot, table_blocks, preferred_element_type=jnp.float32
        ).astype(jnp.bfloat16)
        products = jnp.einsum("tij,tjf->tif", tiles, picked, preferred_element_type=jnp.float32)
        selector = ((targets[None, :] == dest_ids[:, None]) & live[None, :]).astype(jnp.float32)
        return totals + jnp.einsum(
            "qt,tif->qif", selector, products, precision=lax.Precision.HIGHEST
        )

    empty = jnp.zeros((dest_blocks, tile_width, feat_width), jnp.float32)
    return lax.fori_loop(0, rounds, one_round, empty)


def per_device(features, edge_tiles, tile_src, tile_dst, tile_count, weight, out_bias):
    tiles_here = edge_tiles[0, 0]
    source_ids = tile_src[0, 0]
    target_ids = tile_dst[0, 0]
    live_count = tile_count[0, 0]
    slot_total = tiles_here.shape[0]
    tile_width = tiles_here.shape[-1]
    node_rows = features.shape[0]
    feat_width = features.shape[1]
    group_count = lax.axis_size("row")
    dest_blocks = group_count * node_rows // tile_width
    slot_ids = jnp.arange(slot_total, dtype=jnp.int32)
    live_slot = slot_ids < live_count
    table = lax.all_gather(features, "blk", axis=0, tiled=True)
    totals = accumulate(table, source_ids, tiles_here, target_ids, live_slot, dest_blocks).reshape(
        -1, feat_width
    )
    row_sums = jnp.sum(tiles_here, axis=2, dtype=jnp.float32)
    block_ids = jnp.arange(dest_blocks, dtype=jnp.int32)
    selector = ((target_ids[None, :] == block_ids[:, None]) & live_slot[None, :]).astype(
        jnp.float32
    )
    degree_part = jnp.dot(selector, row_sums, precision=lax.Precision.HIGHEST).reshape(-1)
    aggregate, degree = (
        lax.psum_scatter(
            totals.astype(jnp.bfloat16), "row", scatter_dimension=0, tiled=True
        ).astype(jnp.float32),
        lax.psum_scatter(
            degree_part.astype(jnp.bfloat16), "row", scatter_dimension=0, tiled=True
        ).astype(jnp.float32),
    )
    neighbor_mean = (aggregate / jnp.maximum(degree, 1.0)[:, None]).astype(jnp.bfloat16)
    joined = jnp.concatenate([features, neighbor_mean], axis=1)
    mixed = jnp.dot(joined, weight, preferred_element_type=jnp.float32) + out_bias
    return jax.nn.relu(mixed).astype(jnp.bfloat16)


def solution(mesh):
    in_specs = (
        P(("row", "blk"), None),
        P("row", "blk", None, None, None),
        P("row", "blk", None),
        P("row", "blk", None),
        P("row", "blk"),
        P(),
        P(),
    )
    out_specs = P(("row", "blk"), None)

    def body(features, edge_tiles, *rest):
        dense = 2 * lax.axis_size("row") * lax.axis_size("blk") * features.shape[0] ** 2
        run = per_device_fused if dense <= DENSE_LIMIT else per_device
        return run(features, edge_tiles, *rest)

    return jax.shard_map(
        body, mesh=mesh, in_specs=in_specs, out_specs=out_specs, check_vma=False
    )
```

```python
import functools

import jax
import jax.numpy as jnp
from jax import lax
from jax.experimental import pallas as pl
from jax.experimental.pallas import tpu as pltpu
from jax.sharding import PartitionSpec as P

MESH = pl.DeviceIdType.MESH
CHUNK = 128
AHEAD = 2
DENSE_LIMIT = 12 * 2**20


def fused(
    rows_n, spots, live_hbm, src_hbm, dst_hbm, feat_hbm, tiles_hbm, weight_hbm, bias_hbm, out_ref,
    live_ref, src_ref, dst_ref, bias_ref, tab, tiles, chain, dense, weight, mine, acc, mixed, degree, send_buf, recv_buf, lists, list_smem,
    in_sem, own_sem, left_sem, right_sem, far_left_sem, far_right_sem, side_sem, line_recv, side_recv, row_send, row_recv,
):
    slots = tiles.shape[0]
    width = tiles.shape[-1]
    chunks = tab.shape[0]
    node_rows = mine.shape[0]
    feat = mine.shape[1]
    per_node = node_rows // width
    sources = spots * 2 * per_node
    dests = rows_n * per_node
    wide = 2 * per_node
    row = lax.axis_index("row")
    blk = lax.axis_index("blk")
    z = blk // 2
    c = blk % 2
    side = z * 2 + (1 - c)

    barrier = pltpu.get_barrier_semaphore()

    def greet(r, b):
        pl.semaphore_signal(barrier, inc=1, device_id=(r, b), device_id_type=MESH)

    @pl.when(z > 0)
    def _():
        greet(row, blk - 2)

    @pl.when(z < spots - 1)
    def _():
        greet(row, blk + 2)

    @pl.when(z > 1)
    def _():
        greet(row, blk - 4)

    @pl.when(z < spots - 2)
    def _():
        greet(row, blk + 4)

    greet(row, side)
    for step in range(1, rows_n):
        greet((row + step) % rows_n, blk)

    def own_local(k):
        return pltpu.make_async_copy(
            feat_hbm.at[:, pl.ds(pl.multiple_of(k * CHUNK, CHUNK), CHUNK)], tab.at[k, z, c], own_sem.at[k]
        )

    def line_copy(k, p, step, sems):
        slot = tab.at[k, p, c]
        return pltpu.make_async_remote_copy(
            src_ref=slot, dst_ref=slot, send_sem=sems.at[k, p], recv_sem=line_recv.at[k, p],
            device_id=(row, blk + 2 * step), device_id_type=MESH,
        )

    def far_copy(k, step, sems):
        slot = tab.at[k, z, c]
        return pltpu.make_async_remote_copy(
            src_ref=slot, dst_ref=slot, send_sem=sems.at[k], recv_sem=line_recv.at[k, z],
            device_id=(row, blk + 4 * step), device_id_type=MESH,
        )

    def side_copy(k, p):
        slot = tab.at[k, p, c]
        return pltpu.make_async_remote_copy(
            src_ref=slot, dst_ref=slot, send_sem=side_sem.at[k, p], recv_sem=side_recv.at[k, p],
            device_id=(row, side), device_id_type=MESH,
        )

    def side_arrival(k, p):
        slot = tab.at[k, p, 1 - c]
        return pltpu.make_async_remote_copy(
            src_ref=slot, dst_ref=slot, send_sem=side_sem.at[k, p], recv_sem=side_recv.at[k, p],
            device_id=(row, side), device_id_type=MESH,
        )

    def row_copy(k, step):
        peer = (row + step) % rows_n
        return pltpu.make_async_remote_copy(
            src_ref=send_buf.at[k, peer], dst_ref=recv_buf.at[k, row],
            send_sem=row_send.at[k, peer], recv_sem=row_recv.at[k, row],
            device_id=(peer, blk), device_id_type=MESH,
        )

    def row_arrival(k, step):
        peer = (row + step) % rows_n
        return pltpu.make_async_remote_copy(
            src_ref=send_buf.at[k, peer], dst_ref=recv_buf.at[k, peer],
            send_sem=row_send.at[k, peer], recv_sem=row_recv.at[k, peer],
            device_id=(peer, blk), device_id_type=MESH,
        )

    def send_own(k):
        own_local(k).wait()

        @pl.when(z > 1)
        def _():
            far_copy(k, -1, far_left_sem).start()

        @pl.when(z < spots - 2)
        def _():
            far_copy(k, 1, far_right_sem).start()

        @pl.when(z > 0)
        def _():
            line_copy(k, z, -1, left_sem).start()

        @pl.when(z < spots - 1)
        def _():
            line_copy(k, z, 1, right_sem).start()

        side_copy(k, z).start()

    loads = [
        pltpu.make_async_copy(tiles_hbm, tiles, in_sem.at[0]),
        pltpu.make_async_copy(feat_hbm, mine, in_sem.at[1]),
        pltpu.make_async_copy(weight_hbm, weight, in_sem.at[2]),
        pltpu.make_async_copy(bias_hbm, bias_ref, in_sem.at[4]),
        pltpu.make_async_copy(live_hbm, live_ref, in_sem.at[5]),
        pltpu.make_async_copy(src_hbm, src_ref, in_sem.at[6]),
        pltpu.make_async_copy(dst_hbm, dst_ref, in_sem.at[7]),
    ]
    for load in loads[4:]:
        load.start()
    for k in range(chunks):
        own_local(k).start()
    loads[0].start()

    greeted = (
        jnp.where(z > 0, 1, 0) + jnp.where(z < spots - 1, 1, 0) + rows_n
        + jnp.where(z > 1, 1, 0) + jnp.where(z < spots - 2, 1, 0)
    )
    pl.semaphore_wait(barrier, greeted)

    inner = (z > 0) & (z < spots - 1)

    def first_sends(k, carry):
        send_own(k)
        return carry

    lax.fori_loop(0, jnp.where(inner, min(AHEAD, chunks), chunks), first_sends, 0)
    for load in loads[1:4]:
        load.start()
    for load in loads[4:]:
        load.wait()

    list_rows = lists.shape[0] - 1
    lane = lax.broadcasted_iota(jnp.int32, (1, 128), 1)
    place = lax.broadcasted_iota(jnp.int32, (list_rows, 128), 0) * 128 + lax.broadcasted_iota(
        jnp.int32, (list_rows, 128), 1
    )
    live = live_ref[0, 0]

    def one_key(t, carry):
        keys, last = carry
        key = dst_ref[0, 0, t] * sources + src_ref[0, 0, t]
        key = jnp.where(t < live, key, -1)
        return jnp.where(lane == t, key, keys), jnp.where(place == key, t, last)

    keys, last = lax.fori_loop(
        0, slots, one_key,
        (jnp.full((1, 128), -1, jnp.int32), jnp.full((list_rows, 128), slots, jnp.int32)), unroll=8,
    )

    def one_before(u, before):
        key = dst_ref[0, 0, u] * sources + src_ref[0, 0, u]
        key = jnp.where(u < live, key, -2)
        return jnp.where((keys == key) & (lane > u), u, before)

    before = lax.fori_loop(0, slots, one_before, jnp.full((1, 128), slots, jnp.int32), unroll=8)
    lists[pl.ds(0, list_rows), :] = last
    lists[pl.ds(list_rows, 1), :] = before
    to_smem = pltpu.make_async_copy(lists, list_smem, in_sem.at[3])
    to_smem.start()
    chain[slots] = jnp.zeros((width, width), jnp.float32)
    loads[0].wait()
    to_smem.wait()

    def one_link(t, carry):
        chain[t] = tiles[t].astype(jnp.float32) + chain[list_smem[list_rows, t]]
        return carry

    lax.fori_loop(0, slots, one_link, 0, unroll=4)

    def one_dest(q, carry):
        total = jnp.zeros((width, width), jnp.float32)
        for s in range(sources):
            at = q * sources + s
            block = chain[list_smem[at // 128, at % 128]]
            dense[s // wide, pl.ds(pl.multiple_of(q * width, width), width), pl.ds(s % wide * width, width)] = (
                block.astype(jnp.bfloat16)
            )
            total += block
        degrees = jnp.broadcast_to(jnp.sum(total, axis=1, keepdims=True), (width, CHUNK))
        send_buf[chunks, q // per_node, pl.ds(pl.multiple_of(q % per_node * width, width), width), :] = (
            degrees.astype(jnp.bfloat16)
        )
        return carry

    lax.fori_loop(0, dests, one_dest, 0)


    def consume(k, p, first):
        block = tab[k, p].reshape(wide * width, CHUNK)
        product = jnp.dot(dense[p], block, preferred_element_type=jnp.float32)
        if first:
            acc[k] = product
        else:
            acc[k] += product

    def send_rows(k):
        for step in range(1, rows_n):
            row_copy(k, step).start()

    def gather_rows(k):
        total = send_buf[k, row].astype(jnp.float32)
        for step in range(1, rows_n):
            row_arrival(k, step).wait_recv()
            total += recv_buf[k, (row + step) % rows_n].astype(jnp.float32)
        return total

    def forward(k, h):
        @pl.when(z + h < spots)
        def _():
            line_copy(k, z + h, -1, left_sem).wait_recv()
            if h > 1:

                @pl.when(z > 0)
                def _():
                    line_copy(k, z + h, -1, left_sem).start()

            side_copy(k, z + h).start()

        @pl.when(z - h >= 0)
        def _():
            line_copy(k, z - h, 1, right_sem).wait_recv()
            if h > 1:

                @pl.when(z < spots - 1)
                def _():
                    line_copy(k, z - h, 1, right_sem).start()

            side_copy(k, z - h).start()

    def consume_at(k, h):
        if h == 0:
            side_arrival(k, z).wait_recv()
            consume(k, z, True)
            return

        @pl.when(z + h < spots)
        def _():
            side_arrival(k, z + h).wait_recv()
            consume(k, z + h, False)

        @pl.when(z - h >= 0)
        def _():
            side_arrival(k, z - h).wait_recv()
            consume(k, z - h, False)

    def finish_mean(k):
        mean = (gather_rows(k) / degree[...]).astype(jnp.bfloat16)
        part = weight[pl.ds(pl.multiple_of(feat + k * CHUNK, CHUNK), CHUNK), :]
        mixed[...] += jnp.dot(mean, part, preferred_element_type=jnp.float32)

    send_rows(chunks)

    def stage(k, carry):
        forward(k, 1)

        @pl.when(inner & (k + AHEAD < chunks))
        def _():
            send_own(k + AHEAD)

        if spots > 2:
            @pl.when(inner & (k == 0))
            def _():
                forward(k, 2)

            @pl.when(inner & (k + 1 < chunks))
            def _():
                forward(k + 1, 2)

            @pl.when(jnp.logical_not(inner))
            def _():
                forward(k, 2)

        for h in range(spots):
            if h > 2:
                forward(k, h)
            consume_at(k, h)
        send_buf[k] = acc[k].astype(jnp.bfloat16).reshape(rows_n, node_rows, CHUNK)
        send_rows(k)

        @pl.when(k == 0)
        def _():
            for load in loads[1:4]:
                load.wait()
            mixed[...] = (
                jnp.dot(mine[...], weight[pl.ds(0, feat), :], preferred_element_type=jnp.float32) + bias_ref[...]
            )
            degree[...] = jnp.maximum(gather_rows(chunks), 1.0)

        @pl.when(k > 0)
        def _():
            finish_mean(k - 1)

        return carry

    lax.fori_loop(0, chunks, stage, 0)
    finish_mean(chunks - 1)
    out_ref[...] = jnp.maximum(mixed[...], 0.0).astype(jnp.bfloat16)

    def finish(k, carry):
        side_copy(k, z).wait_send()

        @pl.when(z > 0)
        def _():
            line_copy(k, z, -1, left_sem).wait_send()

        @pl.when(z < spots - 1)
        def _():
            line_copy(k, z, 1, right_sem).wait_send()

        @pl.when(z > 1)
        def _():
            far_copy(k, -1, far_left_sem).wait_send()

        @pl.when(z < spots - 2)
        def _():
            far_copy(k, 1, far_right_sem).wait_send()

        for h in range(1, spots):

            @pl.when(z + h < spots)
            def _():
                side_copy(k, z + h).wait_send()
                if h > 1:

                    @pl.when(z > 0)
                    def _():
                        line_copy(k, z + h, -1, left_sem).wait_send()

            @pl.when(z - h >= 0)
            def _():
                side_copy(k, z - h).wait_send()
                if h > 1:

                    @pl.when(z < spots - 1)
                    def _():
                        line_copy(k, z - h, 1, right_sem).wait_send()

        return carry

    lax.fori_loop(0, chunks, finish, 0)

    def finish_rows(k, carry):
        for step in range(1, rows_n):
            row_copy(k, step).wait_send()
        return carry

    lax.fori_loop(0, chunks + 1, finish_rows, 0)


def per_device_fused(features, edge_tiles, tile_src, tile_dst, tile_count, weight, out_bias):
    rows_n = lax.axis_size("row")
    spots = lax.axis_size("blk") // 2
    slots, width = edge_tiles.shape[2], edge_tiles.shape[-1]
    node_rows, feat = features.shape
    chunks = feat // CHUNK
    per_node = node_rows // width
    dests, sources = rows_n * per_node, spots * 2 * per_node
    list_rows = -(-dests * sources // 128)
    dest_rows = rows_n * node_rows
    hbm = pl.BlockSpec(memory_space=pltpu.HBM)
    vmem = pl.BlockSpec(memory_space=pltpu.VMEM)
    dma = pltpu.SemaphoreType.DMA
    return pl.pallas_call(
        functools.partial(fused, rows_n, spots),
        out_shape=jax.ShapeDtypeStruct((node_rows, feat), jnp.bfloat16),
        in_specs=[hbm] * 7,
        out_specs=vmem,
        scratch_shapes=[
            pltpu.SMEM(tile_count.shape, jnp.int32),
            pltpu.SMEM(tile_src.shape, jnp.int32),
            pltpu.SMEM(tile_dst.shape, jnp.int32),
            pltpu.VMEM((1, feat), jnp.float32),
            pltpu.VMEM((chunks, spots, 2, node_rows, CHUNK), jnp.bfloat16),
            pltpu.VMEM((slots, width, width), jnp.bfloat16),
            pltpu.VMEM((slots + 1, width, width), jnp.float32),
            pltpu.VMEM((spots, dest_rows, 2 * node_rows), jnp.bfloat16),
            pltpu.VMEM(weight.shape, jnp.bfloat16),
            pltpu.VMEM((node_rows, feat), jnp.bfloat16),
            pltpu.VMEM((chunks, dest_rows, CHUNK), jnp.float32),
            pltpu.VMEM((node_rows, feat), jnp.float32),
            pltpu.VMEM((node_rows, CHUNK), jnp.float32),
            pltpu.VMEM((chunks + 1, rows_n, node_rows, CHUNK), jnp.bfloat16),
            pltpu.VMEM((chunks + 1, rows_n, node_rows, CHUNK), jnp.bfloat16),
            pltpu.VMEM((list_rows + 1, 128), jnp.int32),
            pltpu.SMEM((list_rows + 1, 128), jnp.int32),
            dma((8,)),
            dma((chunks,)),
            dma((chunks, spots)),
            dma((chunks, spots)),
            dma((chunks,)),
            dma((chunks,)),
            dma((chunks, spots)),
            dma((chunks, spots)),
            dma((chunks, spots)),
            dma((chunks + 1, rows_n)),
            dma((chunks + 1, rows_n)),
        ],
        compiler_params=pltpu.CompilerParams(
            collective_id=0, has_side_effects=True, vmem_limit_bytes=56 * 2**20
        ),
    )(
        tile_count,
        tile_src,
        tile_dst,
        features,
        edge_tiles.reshape(slots, width, width),
        weight,
        out_bias.reshape(1, feat),
    )


def accumulate(table, block_of, tiles_here, target_ids, live_slot, dest_blocks):
    slot_total = tiles_here.shape[0]
    tile_width = tiles_here.shape[-1]
    feat_width = table.shape[1]
    table_blocks = table.reshape(-1, tile_width, feat_width)
    source_total = table_blocks.shape[0]
    step_size = 16
    rounds = slot_total // step_size
    source_ids = jnp.arange(source_total, dtype=jnp.int32)
    dest_ids = jnp.arange(dest_blocks, dtype=jnp.int32)

    def one_round(index, totals):
        first = index * step_size
        tiles = lax.dynamic_slice_in_dim(tiles_here, first, step_size, 0)
        blocks = lax.dynamic_slice_in_dim(block_of, first, step_size, 0)
        targets = lax.dynamic_slice_in_dim(target_ids, first, step_size, 0)
        live = lax.dynamic_slice_in_dim(live_slot, first, step_size, 0)
        one_hot = (blocks[:, None] == source_ids[None, :]).astype(jnp.bfloat16)
        picked = jnp.einsum(
            "tk,kif->tif", one_hot, table_blocks, preferred_element_type=jnp.float32
        ).astype(jnp.bfloat16)
        products = jnp.einsum("tij,tjf->tif", tiles, picked, preferred_element_type=jnp.float32)
        selector = ((targets[None, :] == dest_ids[:, None]) & live[None, :]).astype(jnp.float32)
        return totals + jnp.einsum(
            "qt,tif->qif", selector, products, precision=lax.Precision.HIGHEST
        )

    empty = jnp.zeros((dest_blocks, tile_width, feat_width), jnp.float32)
    return lax.fori_loop(0, rounds, one_round, empty)


def per_device(features, edge_tiles, tile_src, tile_dst, tile_count, weight, out_bias):
    tiles_here = edge_tiles[0, 0]
    source_ids = tile_src[0, 0]
    target_ids = tile_dst[0, 0]
    live_count = tile_count[0, 0]
    slot_total = tiles_here.shape[0]
    tile_width = tiles_here.shape[-1]
    node_rows = features.shape[0]
    feat_width = features.shape[1]
    group_count = lax.axis_size("row")
    dest_blocks = group_count * node_rows // tile_width
    slot_ids = jnp.arange(slot_total, dtype=jnp.int32)
    live_slot = slot_ids < live_count
    table = lax.all_gather(features, "blk", axis=0, tiled=True)
    totals = accumulate(table, source_ids, tiles_here, target_ids, live_slot, dest_blocks).reshape(
        -1, feat_width
    )
    row_sums = jnp.sum(tiles_here, axis=2, dtype=jnp.float32)
    block_ids = jnp.arange(dest_blocks, dtype=jnp.int32)
    selector = ((target_ids[None, :] == block_ids[:, None]) & live_slot[None, :]).astype(
        jnp.float32
    )
    degree_part = jnp.dot(selector, row_sums, precision=lax.Precision.HIGHEST).reshape(-1)
    aggregate, degree = (
        lax.psum_scatter(
            totals.astype(jnp.bfloat16), "row", scatter_dimension=0, tiled=True
        ).astype(jnp.float32),
        lax.psum_scatter(
            degree_part.astype(jnp.bfloat16), "row", scatter_dimension=0, tiled=True
        ).astype(jnp.float32),
    )
    neighbor_mean = (aggregate / jnp.maximum(degree, 1.0)[:, None]).astype(jnp.bfloat16)
    joined = jnp.concatenate([features, neighbor_mean], axis=1)
    mixed = jnp.dot(joined, weight, preferred_element_type=jnp.float32) + out_bias
    return jax.nn.relu(mixed).astype(jnp.bfloat16)


def solution(mesh):
    in_specs = (
        P(("row", "blk"), None),
        P("row", "blk", None, None, None),
        P("row", "blk", None),
        P("row", "blk", None),
        P("row", "blk"),
        P(),
        P(),
    )
    out_specs = P(("row", "blk"), None)

    def body(features, edge_tiles, *rest):
        dense = 2 * lax.axis_size("row") * lax.axis_size("blk") * features.shape[0] ** 2
        run = per_device_fused if dense <= DENSE_LIMIT else per_device
        return run(features, edge_tiles, *rest)

    return jax.shard_map(
        body, mesh=mesh, in_specs=in_specs, out_specs=out_specs, check_vma=False
    )
```

```python
import functools

import jax
import jax.numpy as jnp
from jax import lax
from jax.experimental import pallas as pl
from jax.experimental.pallas import tpu as pltpu
from jax.sharding import PartitionSpec as P

MESH = pl.DeviceIdType.MESH
CHUNK = 128
AHEAD = 3
DENSE_LIMIT = 12 * 2**20


def fused(
    rows_n, spots, live_hbm, src_hbm, dst_hbm, feat_hbm, tiles_hbm, weight_hbm, bias_hbm, out_ref,
    live_ref, src_ref, dst_ref, bias_ref, tab, tiles, chain, dense, weight, mine, acc, mixed, degree, send_buf, recv_buf, lists, list_smem,
    in_sem, own_sem, left_sem, right_sem, far_left_sem, far_right_sem, side_sem, line_recv, side_recv, row_send, row_recv,
):
    slots = tiles.shape[0]
    width = tiles.shape[-1]
    chunks = tab.shape[0]
    node_rows = mine.shape[0]
    feat = mine.shape[1]
    per_node = node_rows // width
    sources = spots * 2 * per_node
    dests = rows_n * per_node
    wide = 2 * per_node
    row = lax.axis_index("row")
    blk = lax.axis_index("blk")
    z = blk // 2
    c = blk % 2
    side = z * 2 + (1 - c)

    barrier = pltpu.get_barrier_semaphore()

    def greet(r, b):
        pl.semaphore_signal(barrier, inc=1, device_id=(r, b), device_id_type=MESH)

    @pl.when(z > 0)
    def _():
        greet(row, blk - 2)

    @pl.when(z < spots - 1)
    def _():
        greet(row, blk + 2)

    @pl.when(z > 1)
    def _():
        greet(row, blk - 4)

    @pl.when(z < spots - 2)
    def _():
        greet(row, blk + 4)

    greet(row, side)
    for step in range(1, rows_n):
        greet((row + step) % rows_n, blk)

    def own_local(k):
        return pltpu.make_async_copy(
            feat_hbm.at[:, pl.ds(pl.multiple_of(k * CHUNK, CHUNK), CHUNK)], tab.at[k, z, c], own_sem.at[k]
        )

    def line_copy(k, p, step, sems):
        slot = tab.at[k, p, c]
        return pltpu.make_async_remote_copy(
            src_ref=slot, dst_ref=slot, send_sem=sems.at[k, p], recv_sem=line_recv.at[k, p],
            device_id=(row, blk + 2 * step), device_id_type=MESH,
        )

    def far_copy(k, step, sems):
        slot = tab.at[k, z, c]
        return pltpu.make_async_remote_copy(
            src_ref=slot, dst_ref=slot, send_sem=sems.at[k], recv_sem=line_recv.at[k, z],
            device_id=(row, blk + 4 * step), device_id_type=MESH,
        )

    def side_copy(k, p):
        slot = tab.at[k, p, c]
        return pltpu.make_async_remote_copy(
            src_ref=slot, dst_ref=slot, send_sem=side_sem.at[k, p], recv_sem=side_recv.at[k, p],
            device_id=(row, side), device_id_type=MESH,
        )

    def side_arrival(k, p):
        slot = tab.at[k, p, 1 - c]
        return pltpu.make_async_remote_copy(
            src_ref=slot, dst_ref=slot, send_sem=side_sem.at[k, p], recv_sem=side_recv.at[k, p],
            device_id=(row, side), device_id_type=MESH,
        )

    def row_copy(k, step):
        peer = (row + step) % rows_n
        return pltpu.make_async_remote_copy(
            src_ref=send_buf.at[k, peer], dst_ref=recv_buf.at[k, row],
            send_sem=row_send.at[k, peer], recv_sem=row_recv.at[k, row],
            device_id=(peer, blk), device_id_type=MESH,
        )

    def row_arrival(k, step):
        peer = (row + step) % rows_n
        return pltpu.make_async_remote_copy(
            src_ref=send_buf.at[k, peer], dst_ref=recv_buf.at[k, peer],
            send_sem=row_send.at[k, peer], recv_sem=row_recv.at[k, peer],
            device_id=(peer, blk), device_id_type=MESH,
        )

    def send_own(k):
        own_local(k).wait()

        @pl.when(z > 0)
        def _():
            line_copy(k, z, -1, left_sem).start()

        @pl.when(z < spots - 1)
        def _():
            line_copy(k, z, 1, right_sem).start()

        @pl.when(z > 1)
        def _():
            far_copy(k, -1, far_left_sem).start()

        @pl.when(z < spots - 2)
        def _():
            far_copy(k, 1, far_right_sem).start()

        side_copy(k, z).start()

    loads = [
        pltpu.make_async_copy(tiles_hbm, tiles, in_sem.at[0]),
        pltpu.make_async_copy(feat_hbm, mine, in_sem.at[1]),
        pltpu.make_async_copy(weight_hbm, weight, in_sem.at[2]),
        pltpu.make_async_copy(bias_hbm, bias_ref, in_sem.at[4]),
        pltpu.make_async_copy(live_hbm, live_ref, in_sem.at[5]),
        pltpu.make_async_copy(src_hbm, src_ref, in_sem.at[6]),
        pltpu.make_async_copy(dst_hbm, dst_ref, in_sem.at[7]),
    ]
    for load in loads[4:]:
        load.start()
    for k in range(chunks):
        own_local(k).start()
    loads[0].start()

    greeted = (
        jnp.where(z > 0, 1, 0) + jnp.where(z < spots - 1, 1, 0) + rows_n
        + jnp.where(z > 1, 1, 0) + jnp.where(z < spots - 2, 1, 0)
    )
    pl.semaphore_wait(barrier, greeted)

    def first_sends(k, carry):
        send_own(k)
        return carry

    lax.fori_loop(0, min(AHEAD, chunks), first_sends, 0)
    for load in loads[1:4]:
        load.start()
    for load in loads[4:]:
        load.wait()

    list_rows = lists.shape[0] - 1
    lane = lax.broadcasted_iota(jnp.int32, (1, 128), 1)
    place = lax.broadcasted_iota(jnp.int32, (list_rows, 128), 0) * 128 + lax.broadcasted_iota(
        jnp.int32, (list_rows, 128), 1
    )
    live = live_ref[0, 0]

    def one_key(t, carry):
        keys, last = carry
        key = dst_ref[0, 0, t] * sources + src_ref[0, 0, t]
        key = jnp.where(t < live, key, -1)
        return jnp.where(lane == t, key, keys), jnp.where(place == key, t, last)

    keys, last = lax.fori_loop(
        0, slots, one_key,
        (jnp.full((1, 128), -1, jnp.int32), jnp.full((list_rows, 128), slots, jnp.int32)), unroll=8,
    )

    def one_before(u, before):
        key = dst_ref[0, 0, u] * sources + src_ref[0, 0, u]
        key = jnp.where(u < live, key, -2)
        return jnp.where((keys == key) & (lane > u), u, before)

    before = lax.fori_loop(0, slots, one_before, jnp.full((1, 128), slots, jnp.int32), unroll=8)
    lists[pl.ds(0, list_rows), :] = last
    lists[pl.ds(list_rows, 1), :] = before
    to_smem = pltpu.make_async_copy(lists, list_smem, in_sem.at[3])
    to_smem.start()
    chain[slots] = jnp.zeros((width, width), jnp.float32)
    loads[0].wait()
    to_smem.wait()

    def one_link(t, carry):
        chain[t] = tiles[t].astype(jnp.float32) + chain[list_smem[list_rows, t]]
        return carry

    lax.fori_loop(0, slots, one_link, 0, unroll=4)

    def one_dest(q, carry):
        total = jnp.zeros((width, width), jnp.float32)
        for s in range(sources):
            at = q * sources + s
            block = chain[list_smem[at // 128, at % 128]]
            dense[s // wide, pl.ds(pl.multiple_of(q * width, width), width), pl.ds(s % wide * width, width)] = (
                block.astype(jnp.bfloat16)
            )
            total += block
        degrees = jnp.broadcast_to(jnp.sum(total, axis=1, keepdims=True), (width, CHUNK))
        send_buf[chunks, q // per_node, pl.ds(pl.multiple_of(q % per_node * width, width), width), :] = (
            degrees.astype(jnp.bfloat16)
        )
        return carry

    lax.fori_loop(0, dests, one_dest, 0)


    def consume(k, p, first):
        block = tab[k, p].reshape(wide * width, CHUNK)
        product = jnp.dot(dense[p], block, preferred_element_type=jnp.float32)
        if first:
            acc[k] = product
        else:
            acc[k] += product

    def send_rows(k):
        for step in range(1, rows_n):
            row_copy(k, step).start()

    def gather_rows(k):
        total = send_buf[k, row].astype(jnp.float32)
        for step in range(1, rows_n):
            row_arrival(k, step).wait_recv()
            total += recv_buf[k, (row + step) % rows_n].astype(jnp.float32)
        return total

    def forward(k, h):
        @pl.when(z + h < spots)
        def _():
            line_copy(k, z + h, -1, left_sem).wait_recv()
            if h > 1:

                @pl.when(z > 0)
                def _():
                    line_copy(k, z + h, -1, left_sem).start()

            side_copy(k, z + h).start()

        @pl.when(z - h >= 0)
        def _():
            line_copy(k, z - h, 1, right_sem).wait_recv()
            if h > 1:

                @pl.when(z < spots - 1)
                def _():
                    line_copy(k, z - h, 1, right_sem).start()

            side_copy(k, z - h).start()

    def consume_at(k, h):
        if h == 0:
            side_arrival(k, z).wait_recv()
            consume(k, z, True)
            return

        @pl.when(z + h < spots)
        def _():
            side_arrival(k, z + h).wait_recv()
            consume(k, z + h, False)

        @pl.when(z - h >= 0)
        def _():
            side_arrival(k, z - h).wait_recv()
            consume(k, z - h, False)

    def finish_mean(k):
        mean = (gather_rows(k) / degree[...]).astype(jnp.bfloat16)
        part = weight[pl.ds(pl.multiple_of(feat + k * CHUNK, CHUNK), CHUNK), :]
        mixed[...] += jnp.dot(mean, part, preferred_element_type=jnp.float32)

    send_rows(chunks)

    def stage(k, carry):
        @pl.when(k + AHEAD < chunks)
        def _():
            send_own(k + AHEAD)

        for h in range(1, min(3, spots)):
            forward(k, h)

        for h in range(spots):
            if h > 2:
                forward(k, h)
            consume_at(k, h)
        send_buf[k] = acc[k].astype(jnp.bfloat16).reshape(rows_n, node_rows, CHUNK)
        send_rows(k)

        @pl.when(k == 0)
        def _():
            for load in loads[1:4]:
                load.wait()
            mixed[...] = (
                jnp.dot(mine[...], weight[pl.ds(0, feat), :], preferred_element_type=jnp.float32) + bias_ref[...]
            )
            degree[...] = jnp.maximum(gather_rows(chunks), 1.0)

        @pl.when(k > 0)
        def _():
            finish_mean(k - 1)

        return carry

    lax.fori_loop(0, chunks, stage, 0)
    finish_mean(chunks - 1)
    out_ref[...] = jnp.maximum(mixed[...], 0.0).astype(jnp.bfloat16)

    def finish(k, carry):
        side_copy(k, z).wait_send()

        @pl.when(z > 0)
        def _():
            line_copy(k, z, -1, left_sem).wait_send()

        @pl.when(z < spots - 1)
        def _():
            line_copy(k, z, 1, right_sem).wait_send()

        @pl.when(z > 1)
        def _():
            far_copy(k, -1, far_left_sem).wait_send()

        @pl.when(z < spots - 2)
        def _():
            far_copy(k, 1, far_right_sem).wait_send()

        for h in range(1, spots):

            @pl.when(z + h < spots)
            def _():
                side_copy(k, z + h).wait_send()
                if h > 1:

                    @pl.when(z > 0)
                    def _():
                        line_copy(k, z + h, -1, left_sem).wait_send()

            @pl.when(z - h >= 0)
            def _():
                side_copy(k, z - h).wait_send()
                if h > 1:

                    @pl.when(z < spots - 1)
                    def _():
                        line_copy(k, z - h, 1, right_sem).wait_send()

        return carry

    lax.fori_loop(0, chunks, finish, 0)

    def finish_rows(k, carry):
        for step in range(1, rows_n):
            row_copy(k, step).wait_send()
        return carry

    lax.fori_loop(0, chunks + 1, finish_rows, 0)


def per_device_fused(features, edge_tiles, tile_src, tile_dst, tile_count, weight, out_bias):
    rows_n = lax.axis_size("row")
    spots = lax.axis_size("blk") // 2
    slots, width = edge_tiles.shape[2], edge_tiles.shape[-1]
    node_rows, feat = features.shape
    chunks = feat // CHUNK
    per_node = node_rows // width
    dests, sources = rows_n * per_node, spots * 2 * per_node
    list_rows = -(-dests * sources // 128)
    dest_rows = rows_n * node_rows
    hbm = pl.BlockSpec(memory_space=pltpu.HBM)
    vmem = pl.BlockSpec(memory_space=pltpu.VMEM)
    dma = pltpu.SemaphoreType.DMA
    return pl.pallas_call(
        functools.partial(fused, rows_n, spots),
        out_shape=jax.ShapeDtypeStruct((node_rows, feat), jnp.bfloat16),
        in_specs=[hbm] * 7,
        out_specs=vmem,
        scratch_shapes=[
            pltpu.SMEM(tile_count.shape, jnp.int32),
            pltpu.SMEM(tile_src.shape, jnp.int32),
            pltpu.SMEM(tile_dst.shape, jnp.int32),
            pltpu.VMEM((1, feat), jnp.float32),
            pltpu.VMEM((chunks, spots, 2, node_rows, CHUNK), jnp.bfloat16),
            pltpu.VMEM((slots, width, width), jnp.bfloat16),
            pltpu.VMEM((slots + 1, width, width), jnp.float32),
            pltpu.VMEM((spots, dest_rows, 2 * node_rows), jnp.bfloat16),
            pltpu.VMEM(weight.shape, jnp.bfloat16),
            pltpu.VMEM((node_rows, feat), jnp.bfloat16),
            pltpu.VMEM((chunks, dest_rows, CHUNK), jnp.float32),
            pltpu.VMEM((node_rows, feat), jnp.float32),
            pltpu.VMEM((node_rows, CHUNK), jnp.float32),
            pltpu.VMEM((chunks + 1, rows_n, node_rows, CHUNK), jnp.bfloat16),
            pltpu.VMEM((chunks + 1, rows_n, node_rows, CHUNK), jnp.bfloat16),
            pltpu.VMEM((list_rows + 1, 128), jnp.int32),
            pltpu.SMEM((list_rows + 1, 128), jnp.int32),
            dma((8,)),
            dma((chunks,)),
            dma((chunks, spots)),
            dma((chunks, spots)),
            dma((chunks,)),
            dma((chunks,)),
            dma((chunks, spots)),
            dma((chunks, spots)),
            dma((chunks, spots)),
            dma((chunks + 1, rows_n)),
            dma((chunks + 1, rows_n)),
        ],
        compiler_params=pltpu.CompilerParams(
            collective_id=0, has_side_effects=True, vmem_limit_bytes=56 * 2**20
        ),
    )(
        tile_count,
        tile_src,
        tile_dst,
        features,
        edge_tiles.reshape(slots, width, width),
        weight,
        out_bias.reshape(1, feat),
    )


def accumulate(table, block_of, tiles_here, target_ids, live_slot, dest_blocks):
    slot_total = tiles_here.shape[0]
    tile_width = tiles_here.shape[-1]
    feat_width = table.shape[1]
    table_blocks = table.reshape(-1, tile_width, feat_width)
    source_total = table_blocks.shape[0]
    step_size = 16
    rounds = slot_total // step_size
    source_ids = jnp.arange(source_total, dtype=jnp.int32)
    dest_ids = jnp.arange(dest_blocks, dtype=jnp.int32)

    def one_round(index, totals):
        first = index * step_size
        tiles = lax.dynamic_slice_in_dim(tiles_here, first, step_size, 0)
        blocks = lax.dynamic_slice_in_dim(block_of, first, step_size, 0)
        targets = lax.dynamic_slice_in_dim(target_ids, first, step_size, 0)
        live = lax.dynamic_slice_in_dim(live_slot, first, step_size, 0)
        one_hot = (blocks[:, None] == source_ids[None, :]).astype(jnp.bfloat16)
        picked = jnp.einsum(
            "tk,kif->tif", one_hot, table_blocks, preferred_element_type=jnp.float32
        ).astype(jnp.bfloat16)
        products = jnp.einsum("tij,tjf->tif", tiles, picked, preferred_element_type=jnp.float32)
        selector = ((targets[None, :] == dest_ids[:, None]) & live[None, :]).astype(jnp.float32)
        return totals + jnp.einsum(
            "qt,tif->qif", selector, products, precision=lax.Precision.HIGHEST
        )

    empty = jnp.zeros((dest_blocks, tile_width, feat_width), jnp.float32)
    return lax.fori_loop(0, rounds, one_round, empty)


def per_device(features, edge_tiles, tile_src, tile_dst, tile_count, weight, out_bias):
    tiles_here = edge_tiles[0, 0]
    source_ids = tile_src[0, 0]
    target_ids = tile_dst[0, 0]
    live_count = tile_count[0, 0]
    slot_total = tiles_here.shape[0]
    tile_width = tiles_here.shape[-1]
    node_rows = features.shape[0]
    feat_width = features.shape[1]
    group_count = lax.axis_size("row")
    dest_blocks = group_count * node_rows // tile_width
    slot_ids = jnp.arange(slot_total, dtype=jnp.int32)
    live_slot = slot_ids < live_count
    table = lax.all_gather(features, "blk", axis=0, tiled=True)
    totals = accumulate(table, source_ids, tiles_here, target_ids, live_slot, dest_blocks).reshape(
        -1, feat_width
    )
    row_sums = jnp.sum(tiles_here, axis=2, dtype=jnp.float32)
    block_ids = jnp.arange(dest_blocks, dtype=jnp.int32)
    selector = ((target_ids[None, :] == block_ids[:, None]) & live_slot[None, :]).astype(
        jnp.float32
    )
    degree_part = jnp.dot(selector, row_sums, precision=lax.Precision.HIGHEST).reshape(-1)
    aggregate, degree = (
        lax.psum_scatter(
            totals.astype(jnp.bfloat16), "row", scatter_dimension=0, tiled=True
        ).astype(jnp.float32),
        lax.psum_scatter(
            degree_part.astype(jnp.bfloat16), "row", scatter_dimension=0, tiled=True
        ).astype(jnp.float32),
    )
    neighbor_mean = (aggregate / jnp.maximum(degree, 1.0)[:, None]).astype(jnp.bfloat16)
    joined = jnp.concatenate([features, neighbor_mean], axis=1)
    mixed = jnp.dot(joined, weight, preferred_element_type=jnp.float32) + out_bias
    return jax.nn.relu(mixed).astype(jnp.bfloat16)


def solution(mesh):
    in_specs = (
        P(("row", "blk"), None),
        P("row", "blk", None, None, None),
        P("row", "blk", None),
        P("row", "blk", None),
        P("row", "blk"),
        P(),
        P(),
    )
    out_specs = P(("row", "blk"), None)

    def body(features, edge_tiles, *rest):
        dense = 2 * lax.axis_size("row") * lax.axis_size("blk") * features.shape[0] ** 2
        run = per_device_fused if dense <= DENSE_LIMIT else per_device
        return run(features, edge_tiles, *rest)

    return jax.shard_map(
        body, mesh=mesh, in_specs=in_specs, out_specs=out_specs, check_vma=False
    )
```

```python
import functools

import jax
import jax.numpy as jnp
from jax import lax
from jax.experimental import pallas as pl
from jax.experimental.pallas import tpu as pltpu
from jax.sharding import PartitionSpec as P

MESH = pl.DeviceIdType.MESH
CHUNK = 128
AHEAD = 2
FAR = 3
DENSE_LIMIT = 12 * 2**20


def fused(
    rows_n, spots, live_hbm, src_hbm, dst_hbm, feat_hbm, tiles_hbm, weight_hbm, bias_hbm, out_ref,
    live_ref, src_ref, dst_ref, bias_ref, tab, tiles, chain, dense, weight, mine, acc, mixed, degree, send_buf, recv_buf, lists, list_smem,
    in_sem, own_sem, left_sem, right_sem, far_left_sem, far_right_sem, side_sem, line_recv, side_recv, row_send, row_recv,
):
    slots = tiles.shape[0]
    width = tiles.shape[-1]
    chunks = tab.shape[0]
    node_rows = mine.shape[0]
    feat = mine.shape[1]
    per_node = node_rows // width
    sources = spots * 2 * per_node
    dests = rows_n * per_node
    wide = 2 * per_node
    row = lax.axis_index("row")
    blk = lax.axis_index("blk")
    z = blk // 2
    c = blk % 2
    side = z * 2 + (1 - c)

    barrier = pltpu.get_barrier_semaphore()

    def greet(r, b):
        pl.semaphore_signal(barrier, inc=1, device_id=(r, b), device_id_type=MESH)

    @pl.when(z > 0)
    def _():
        greet(row, blk - 2)

    @pl.when(z < spots - 1)
    def _():
        greet(row, blk + 2)

    @pl.when(z > 1)
    def _():
        greet(row, blk - 4)

    @pl.when(z < spots - 2)
    def _():
        greet(row, blk + 4)

    greet(row, side)
    for step in range(1, rows_n):
        greet((row + step) % rows_n, blk)

    def own_local(k):
        return pltpu.make_async_copy(
            feat_hbm.at[:, pl.ds(pl.multiple_of(k * CHUNK, CHUNK), CHUNK)], tab.at[k, z, c], own_sem.at[k]
        )

    def line_copy(k, p, step, sems):
        slot = tab.at[k, p, c]
        return pltpu.make_async_remote_copy(
            src_ref=slot, dst_ref=slot, send_sem=sems.at[k, p], recv_sem=line_recv.at[k, p],
            device_id=(row, blk + 2 * step), device_id_type=MESH,
        )

    def far_copy(k, step, sems):
        slot = tab.at[k, z, c]
        return pltpu.make_async_remote_copy(
            src_ref=slot, dst_ref=slot, send_sem=sems.at[k], recv_sem=line_recv.at[k, z],
            device_id=(row, blk + 4 * step), device_id_type=MESH,
        )

    def side_copy(k, p):
        slot = tab.at[k, p, c]
        return pltpu.make_async_remote_copy(
            src_ref=slot, dst_ref=slot, send_sem=side_sem.at[k, p], recv_sem=side_recv.at[k, p],
            device_id=(row, side), device_id_type=MESH,
        )

    def side_arrival(k, p):
        slot = tab.at[k, p, 1 - c]
        return pltpu.make_async_remote_copy(
            src_ref=slot, dst_ref=slot, send_sem=side_sem.at[k, p], recv_sem=side_recv.at[k, p],
            device_id=(row, side), device_id_type=MESH,
        )

    def row_copy(k, step):
        peer = (row + step) % rows_n
        return pltpu.make_async_remote_copy(
            src_ref=send_buf.at[k, peer], dst_ref=recv_buf.at[k, row],
            send_sem=row_send.at[k, peer], recv_sem=row_recv.at[k, row],
            device_id=(peer, blk), device_id_type=MESH,
        )

    def row_arrival(k, step):
        peer = (row + step) % rows_n
        return pltpu.make_async_remote_copy(
            src_ref=send_buf.at[k, peer], dst_ref=recv_buf.at[k, peer],
            send_sem=row_send.at[k, peer], recv_sem=row_recv.at[k, peer],
            device_id=(peer, blk), device_id_type=MESH,
        )

    def send_own(k):
        own_local(k).wait()

        @pl.when(z > 0)
        def _():
            line_copy(k, z, -1, left_sem).start()

        @pl.when(z < spots - 1)
        def _():
            line_copy(k, z, 1, right_sem).start()

        @pl.when((z > 1) & (k < FAR))
        def _():
            far_copy(k, -1, far_left_sem).start()

        @pl.when((z < spots - 2) & (k < FAR))
        def _():
            far_copy(k, 1, far_right_sem).start()

        side_copy(k, z).start()

    loads = [
        pltpu.make_async_copy(tiles_hbm, tiles, in_sem.at[0]),
        pltpu.make_async_copy(feat_hbm, mine, in_sem.at[1]),
        pltpu.make_async_copy(weight_hbm, weight, in_sem.at[2]),
        pltpu.make_async_copy(bias_hbm, bias_ref, in_sem.at[4]),
        pltpu.make_async_copy(live_hbm, live_ref, in_sem.at[5]),
        pltpu.make_async_copy(src_hbm, src_ref, in_sem.at[6]),
        pltpu.make_async_copy(dst_hbm, dst_ref, in_sem.at[7]),
    ]
    for load in loads[4:]:
        load.start()
    for k in range(chunks):
        own_local(k).start()
    loads[0].start()

    greeted = (
        jnp.where(z > 0, 1, 0) + jnp.where(z < spots - 1, 1, 0) + rows_n
        + jnp.where(z > 1, 1, 0) + jnp.where(z < spots - 2, 1, 0)
    )
    pl.semaphore_wait(barrier, greeted)

    def first_sends(k, carry):
        send_own(k)
        return carry

    lax.fori_loop(0, min(AHEAD, chunks), first_sends, 0)
    for load in loads[1:4]:
        load.start()
    for load in loads[4:]:
        load.wait()

    list_rows = lists.shape[0] - 1
    lane = lax.broadcasted_iota(jnp.int32, (1, 128), 1)
    place = lax.broadcasted_iota(jnp.int32, (list_rows, 128), 0) * 128 + lax.broadcasted_iota(
        jnp.int32, (list_rows, 128), 1
    )
    live = live_ref[0, 0]

    def one_key(t, carry):
        keys, last = carry
        key = dst_ref[0, 0, t] * sources + src_ref[0, 0, t]
        key = jnp.where(t < live, key, -1)
        return jnp.where(lane == t, key, keys), jnp.where(place == key, t, last)

    keys, last = lax.fori_loop(
        0, slots, one_key,
        (jnp.full((1, 128), -1, jnp.int32), jnp.full((list_rows, 128), slots, jnp.int32)), unroll=8,
    )

    def one_before(u, before):
        key = dst_ref[0, 0, u] * sources + src_ref[0, 0, u]
        key = jnp.where(u < live, key, -2)
        return jnp.where((keys == key) & (lane > u), u, before)

    before = lax.fori_loop(0, slots, one_before, jnp.full((1, 128), slots, jnp.int32), unroll=8)
    lists[pl.ds(0, list_rows), :] = last
    lists[pl.ds(list_rows, 1), :] = before
    to_smem = pltpu.make_async_copy(lists, list_smem, in_sem.at[3])
    to_smem.start()
    chain[slots] = jnp.zeros((width, width), jnp.float32)
    loads[0].wait()
    to_smem.wait()

    def one_link(t, carry):
        chain[t] = tiles[t].astype(jnp.float32) + chain[list_smem[list_rows, t]]
        return carry

    lax.fori_loop(0, slots, one_link, 0, unroll=4)

    def one_dest(q, carry):
        total = jnp.zeros((width, width), jnp.float32)
        for s in range(sources):
            at = q * sources + s
            block = chain[list_smem[at // 128, at % 128]]
            dense[s // wide, pl.ds(pl.multiple_of(q * width, width), width), pl.ds(s % wide * width, width)] = (
                block.astype(jnp.bfloat16)
            )
            total += block
        degrees = jnp.broadcast_to(jnp.sum(total, axis=1, keepdims=True), (width, CHUNK))
        send_buf[chunks, q // per_node, pl.ds(pl.multiple_of(q % per_node * width, width), width), :] = (
            degrees.astype(jnp.bfloat16)
        )
        return carry

    lax.fori_loop(0, dests, one_dest, 0)


    def consume(k, p, first):
        block = tab[k, p].reshape(wide * width, CHUNK)
        product = jnp.dot(dense[p], block, preferred_element_type=jnp.float32)
        if first:
            acc[k] = product
        else:
            acc[k] += product

    def send_rows(k):
        for step in range(1, rows_n):
            row_copy(k, step).start()

    def gather_rows(k):
        total = send_buf[k, row].astype(jnp.float32)
        for step in range(1, rows_n):
            row_arrival(k, step).wait_recv()
            total += recv_buf[k, (row + step) % rows_n].astype(jnp.float32)
        return total

    def handed(k, h):
        return (k >= FAR) | (h > 1)

    def forward(k, h):
        @pl.when(z + h < spots)
        def _():
            line_copy(k, z + h, -1, left_sem).wait_recv()

            @pl.when((z > 0) & handed(k, h))
            def _():
                line_copy(k, z + h, -1, left_sem).start()

            side_copy(k, z + h).start()

        @pl.when(z - h >= 0)
        def _():
            line_copy(k, z - h, 1, right_sem).wait_recv()

            @pl.when((z < spots - 1) & handed(k, h))
            def _():
                line_copy(k, z - h, 1, right_sem).start()

            side_copy(k, z - h).start()

    def consume_at(k, h):
        if h == 0:
            side_arrival(k, z).wait_recv()
            consume(k, z, True)
            return

        @pl.when(z + h < spots)
        def _():
            side_arrival(k, z + h).wait_recv()
            consume(k, z + h, False)

        @pl.when(z - h >= 0)
        def _():
            side_arrival(k, z - h).wait_recv()
            consume(k, z - h, False)

    def finish_mean(k):
        mean = (gather_rows(k) / degree[...]).astype(jnp.bfloat16)
        part = weight[pl.ds(pl.multiple_of(feat + k * CHUNK, CHUNK), CHUNK), :]
        mixed[...] += jnp.dot(mean, part, preferred_element_type=jnp.float32)

    send_rows(chunks)
    def pass_on(k):
        for h in range(1, min(3, spots)):
            forward(k, h)

        @pl.when(k + AHEAD < chunks)
        def _():
            send_own(k + AHEAD)

    def stage(k, carry):
        pass_on(k)
        for h in range(spots):
            if h > 2:
                forward(k, h)
            consume_at(k, h)
        send_buf[k] = acc[k].astype(jnp.bfloat16).reshape(rows_n, node_rows, CHUNK)
        send_rows(k)

        @pl.when(k == 0)
        def _():
            for load in loads[1:4]:
                load.wait()
            mixed[...] = (
                jnp.dot(mine[...], weight[pl.ds(0, feat), :], preferred_element_type=jnp.float32) + bias_ref[...]
            )
            degree[...] = jnp.maximum(gather_rows(chunks), 1.0)

        @pl.when(k > 0)
        def _():
            finish_mean(k - 1)

        return carry

    lax.fori_loop(0, chunks, stage, 0)
    finish_mean(chunks - 1)
    out_ref[...] = mixed[...].astype(jnp.bfloat16)

    def finish(k, carry):
        side_copy(k, z).wait_send()

        @pl.when(z > 0)
        def _():
            line_copy(k, z, -1, left_sem).wait_send()

        @pl.when(z < spots - 1)
        def _():
            line_copy(k, z, 1, right_sem).wait_send()

        @pl.when((z > 1) & (k < FAR))
        def _():
            far_copy(k, -1, far_left_sem).wait_send()

        @pl.when((z < spots - 2) & (k < FAR))
        def _():
            far_copy(k, 1, far_right_sem).wait_send()

        for h in range(1, spots):

            @pl.when(z + h < spots)
            def _():
                side_copy(k, z + h).wait_send()

                @pl.when((z > 0) & handed(k, h))
                def _():
                    line_copy(k, z + h, -1, left_sem).wait_send()

            @pl.when(z - h >= 0)
            def _():
                side_copy(k, z - h).wait_send()

                @pl.when((z < spots - 1) & handed(k, h))
                def _():
                    line_copy(k, z - h, 1, right_sem).wait_send()

        return carry

    lax.fori_loop(0, chunks, finish, 0)

    def finish_rows(k, carry):
        for step in range(1, rows_n):
            row_copy(k, step).wait_send()
        return carry

    lax.fori_loop(0, chunks + 1, finish_rows, 0)


def per_device_fused(features, edge_tiles, tile_src, tile_dst, tile_count, weight, out_bias):
    rows_n = lax.axis_size("row")
    spots = lax.axis_size("blk") // 2
    slots, width = edge_tiles.shape[2], edge_tiles.shape[-1]
    node_rows, feat = features.shape
    chunks = feat // CHUNK
    per_node = node_rows // width
    dests, sources = rows_n * per_node, spots * 2 * per_node
    list_rows = -(-dests * sources // 128)
    dest_rows = rows_n * node_rows
    hbm = pl.BlockSpec(memory_space=pltpu.HBM)
    vmem = pl.BlockSpec(memory_space=pltpu.VMEM)
    dma = pltpu.SemaphoreType.DMA
    mixed = pl.pallas_call(
        functools.partial(fused, rows_n, spots),
        out_shape=jax.ShapeDtypeStruct((node_rows, feat), jnp.bfloat16),
        in_specs=[hbm] * 7,
        out_specs=vmem,
        scratch_shapes=[
            pltpu.SMEM(tile_count.shape, jnp.int32),
            pltpu.SMEM(tile_src.shape, jnp.int32),
            pltpu.SMEM(tile_dst.shape, jnp.int32),
            pltpu.VMEM((1, feat), jnp.float32),
            pltpu.VMEM((chunks, spots, 2, node_rows, CHUNK), jnp.bfloat16),
            pltpu.VMEM((slots, width, width), jnp.bfloat16),
            pltpu.VMEM((slots + 1, width, width), jnp.float32),
            pltpu.VMEM((spots, dest_rows, 2 * node_rows), jnp.bfloat16),
            pltpu.VMEM(weight.shape, jnp.bfloat16),
            pltpu.VMEM((node_rows, feat), jnp.bfloat16),
            pltpu.VMEM((chunks, dest_rows, CHUNK), jnp.float32),
            pltpu.VMEM((node_rows, feat), jnp.float32),
            pltpu.VMEM((node_rows, CHUNK), jnp.float32),
            pltpu.VMEM((chunks + 1, rows_n, node_rows, CHUNK), jnp.bfloat16),
            pltpu.VMEM((chunks + 1, rows_n, node_rows, CHUNK), jnp.bfloat16),
            pltpu.VMEM((list_rows + 1, 128), jnp.int32),
            pltpu.SMEM((list_rows + 1, 128), jnp.int32),
            dma((8,)),
            dma((chunks,)),
            dma((chunks, spots)),
            dma((chunks, spots)),
            dma((chunks,)),
            dma((chunks,)),
            dma((chunks, spots)),
            dma((chunks, spots)),
            dma((chunks, spots)),
            dma((chunks + 1, rows_n)),
            dma((chunks + 1, rows_n)),
        ],
        compiler_params=pltpu.CompilerParams(
            collective_id=0, has_side_effects=True, vmem_limit_bytes=56 * 2**20
        ),
    )(
        tile_count,
        tile_src,
        tile_dst,
        features,
        edge_tiles.reshape(slots, width, width),
        weight,
        out_bias.reshape(1, feat),
    )
    return jax.nn.relu(mixed)


def accumulate(table, block_of, tiles_here, target_ids, live_slot, dest_blocks):
    slot_total = tiles_here.shape[0]
    tile_width = tiles_here.shape[-1]
    feat_width = table.shape[1]
    table_blocks = table.reshape(-1, tile_width, feat_width)
    source_total = table_blocks.shape[0]
    step_size = 16
    rounds = slot_total // step_size
    source_ids = jnp.arange(source_total, dtype=jnp.int32)
    dest_ids = jnp.arange(dest_blocks, dtype=jnp.int32)

    def one_round(index, totals):
        first = index * step_size
        tiles = lax.dynamic_slice_in_dim(tiles_here, first, step_size, 0)
        blocks = lax.dynamic_slice_in_dim(block_of, first, step_size, 0)
        targets = lax.dynamic_slice_in_dim(target_ids, first, step_size, 0)
        live = lax.dynamic_slice_in_dim(live_slot, first, step_size, 0)
        one_hot = (blocks[:, None] == source_ids[None, :]).astype(jnp.bfloat16)
        picked = jnp.einsum(
            "tk,kif->tif", one_hot, table_blocks, preferred_element_type=jnp.float32
        ).astype(jnp.bfloat16)
        products = jnp.einsum("tij,tjf->tif", tiles, picked, preferred_element_type=jnp.float32)
        selector = ((targets[None, :] == dest_ids[:, None]) & live[None, :]).astype(jnp.float32)
        return totals + jnp.einsum(
            "qt,tif->qif", selector, products, precision=lax.Precision.HIGHEST
        )

    empty = jnp.zeros((dest_blocks, tile_width, feat_width), jnp.float32)
    return lax.fori_loop(0, rounds, one_round, empty)


def per_device(features, edge_tiles, tile_src, tile_dst, tile_count, weight, out_bias):
    tiles_here = edge_tiles[0, 0]
    source_ids = tile_src[0, 0]
    target_ids = tile_dst[0, 0]
    live_count = tile_count[0, 0]
    slot_total = tiles_here.shape[0]
    tile_width = tiles_here.shape[-1]
    node_rows = features.shape[0]
    feat_width = features.shape[1]
    group_count = lax.axis_size("row")
    dest_blocks = group_count * node_rows // tile_width
    slot_ids = jnp.arange(slot_total, dtype=jnp.int32)
    live_slot = slot_ids < live_count
    table = lax.all_gather(features, "blk", axis=0, tiled=True)
    totals = accumulate(table, source_ids, tiles_here, target_ids, live_slot, dest_blocks).reshape(
        -1, feat_width
    )
    row_sums = jnp.sum(tiles_here, axis=2, dtype=jnp.float32)
    block_ids = jnp.arange(dest_blocks, dtype=jnp.int32)
    selector = ((target_ids[None, :] == block_ids[:, None]) & live_slot[None, :]).astype(
        jnp.float32
    )
    degree_part = jnp.dot(selector, row_sums, precision=lax.Precision.HIGHEST).reshape(-1)
    aggregate, degree = (
        lax.psum_scatter(
            totals.astype(jnp.bfloat16), "row", scatter_dimension=0, tiled=True
        ).astype(jnp.float32),
        lax.psum_scatter(
            degree_part.astype(jnp.bfloat16), "row", scatter_dimension=0, tiled=True
        ).astype(jnp.float32),
    )
    neighbor_mean = (aggregate / jnp.maximum(degree, 1.0)[:, None]).astype(jnp.bfloat16)
    joined = jnp.concatenate([features, neighbor_mean], axis=1)
    mixed = jnp.dot(joined, weight, preferred_element_type=jnp.float32) + out_bias
    return jax.nn.relu(mixed).astype(jnp.bfloat16)


def solution(mesh):
    in_specs = (
        P(("row", "blk"), None),
        P("row", "blk", None, None, None),
        P("row", "blk", None),
        P("row", "blk", None),
        P("row", "blk"),
        P(),
        P(),
    )
    out_specs = P(("row", "blk"), None)

    def body(features, edge_tiles, *rest):
        dense = 2 * lax.axis_size("row") * lax.axis_size("blk") * features.shape[0] ** 2
        run = per_device_fused if dense <= DENSE_LIMIT else per_device
        return run(features, edge_tiles, *rest)

    return jax.shard_map(
        body, mesh=mesh, in_specs=in_specs, out_specs=out_specs, check_vma=False
    )
```
